256 devices in a mesh: cuts: 4 (over y_hi, core), fsdp: 64 (over y_lo, z, x).
Axes of the slice: x: 4, y: 4 (y_hi: 2, y_lo: 2; y = y_hi * 2 + y_lo), z: 8, core: 2. Of those that a mesh axis runs over, the one named last changes fastest.
Arguments:
- hid_shared: bfloat16 [196608, 1536], P(('cuts', 'fsdp')), may hold values from -24 to 24
- hid_routed: bfloat16 [24576, 768], P(('cuts', 'fsdp')), may hold values from -96 to 96
- out_grad: bfloat16 [196608, 2560], P(('cuts', 'fsdp')), may hold values from -0.040527344 to 0.040527344
- slot_token: int32 [24576], P(('cuts', 'fsdp')), may hold values from 0 to 767, as said below
- slot_count: int32 [256], P(('cuts', 'fsdp')), may hold values from 24 to 96, as said below
- master_shared: float32 [1536, 2560], P(('cuts', 'fsdp')), may hold values from -6 to 6
- moment_shared: float32 [1536, 2560], P(('cuts', 'fsdp')), may hold values from -1.8 to 1.8
- second_shared: float32 [1536, 2560], P(('cuts', 'fsdp')), may hold values from 0.01 to 1
- master_routed: float32 [768, 2560], P(('cuts', 'fsdp')), may hold values from -6 to 6
- moment_routed: float32 [768, 2560], P(('cuts', 'fsdp')), may hold values from -1.8 to 1.8
- second_routed: float32 [768, 2560], P(('cuts', 'fsdp')), may hold values from 0.01 to 1
Outputs:
- new_moment_shared: float32 [1536, 2560], P(('cuts', 'fsdp'))
- new_second_shared: float32 [1536, 2560], P(('cuts', 'fsdp'))
- new_moment_routed: float32 [768, 2560], P(('cuts', 'fsdp'))
- new_second_routed: float32 [768, 2560], P(('cuts', 'fsdp'))
- weight_shared: bfloat16 [1536, 2560], P('cuts')
- weight_routed: bfloat16 [768, 2560], P('cuts')
The draws below stay inside these ranges and needn't reach their ends.
Inputs may be any that keep to these rules, and one draw needn't show every extreme that they name: `slot_token`: within one device the 96 slots name distinct tokens of that device. `slot_count`: at least one device has all 96 slots live.
All inputs are finite; a program needn't handle non-finite values.
Results may differ from the reference program's by a relative error of at most 0.001.
Values may be sent and summed in bfloat16 or wider, within the bound.
No kernel may reach another device: no remote copies, remote signals or barrier semaphores. Data moves between devices by JAX's collectives and lax.ppermute only.
A program may use at most 192 MiB of HBM per device.

```python
import math
import jax
import jax.numpy as jnp

D_W = 2560
HS = 1536
RH = 768
TOK_DEV = 768
CAP = 96
SENDERS = 256
TOKENS = 196608
SLOTS = 24576


def draw_slot_token(key, part):
    key = jax.random.fold_in(key, 11)
    keys = jax.random.split(key, SENDERS)
    picked = jax.vmap(lambda k: jax.random.permutation(k, TOK_DEV)[:CAP])(keys)
    return picked.reshape(-1).astype(jnp.int32)


def draw_slot_count(key, part):
    key = jax.random.fold_in(key, 23)
    base = jax.random.randint(key, (SENDERS,), CAP // 4, CAP + 1)
    chosen = jax.random.randint(jax.random.fold_in(key, 5), (), 0, SENDERS)
    filled = jnp.arange(SENDERS, dtype=jnp.int32) == chosen
    return jnp.where(filled, CAP, base).astype(jnp.int32)


def raised(values, key, source, target, blocks, factor):
    def block_of(dim):
        return (jnp.arange(values.shape[dim]) // (values.shape[dim] // blocks)).reshape((-1,) + (1,) * (values.ndim - 1 - dim))

    near = jax.random.permutation(key, blocks)[block_of(target)]
    far = (block_of(target) + blocks // 2) % blocks
    return jnp.where((block_of(source) == near) | (block_of(source) == far), factor * values, values)


def steps_of(stream_key, extent, shards, smallest, top_value):
    def one(position, shards_of):
        draws = jax.random.uniform(jax.random.fold_in(jax.random.fold_in(stream_key, 6), position), (shards_of,), jnp.float32, smallest / len(shards), top_value / len(shards))
        return jnp.repeat(jnp.exp(draws), extent[position] // shards_of).reshape((-1,) + (1,) * (len(extent) - position - 1))

    gain = one(*shards[0])
    for cut in shards[1:]:
        gain = gain * one(*cut)
    return gain


def gaussian(own_key, extent, spread, most, pieces=(), kind=jnp.bfloat16):
    array = jax.random.normal(own_key, extent, jnp.float32) * spread
    if len(pieces) > 0:
        array = steps_of(own_key, extent, pieces, -0.22, 0.18) * array
    return jnp.clip(array, min=-most, max=most).astype(kind)


def noise_with(stream_key, dims, deviation, limit, cuts, heavy, kind=jnp.bfloat16):
    drawn = deviation * jax.random.normal(stream_key, dims, jnp.float32)
    if cuts:
        drawn = drawn * steps_of(stream_key, dims, cuts, -0.22, 0.18)
    return jnp.clip(raised(drawn, jax.random.fold_in(stream_key, 3), *heavy), -limit, limit).astype(kind)


def setup_inputs(seed: int = 0) -> dict:
    key_list = jax.random.split(jax.random.key(seed), 12)
    return {
        "hid_shared": noise_with(key_list[0], (TOKENS, HS), 1.0, 24.0, ((0, 256),), (0, 1, 256, 6.0)),
        "hid_routed": noise_with(key_list[1], (SLOTS, RH), (1.3 * (TOK_DEV / CAP) ** 0.5), 96.0, ((0, 256),), (0, 1, 256, 6.0)),
        "out_grad": gaussian(key_list[2], (TOKENS, D_W), (3.0 / TOKENS ** 0.5), 0.040527344, ((0, 256),)),
        "slot_token": draw_slot_token(jax.random.fold_in(key_list[11], 71), 0),
        "slot_count": draw_slot_count(jax.random.fold_in(key_list[11], 71), 0),
        "master_shared": gaussian(key_list[5], (HS, D_W), 1.0, 6.0, ((0, 256),), jnp.float32),
        "moment_shared": gaussian(key_list[6], (HS, D_W), 0.3, 1.8, ((0, 256),), jnp.float32),
        "second_shared": jnp.clip(jnp.exp(math.log(1.0) - 4.6051702 * jax.random.uniform(key_list[7], (HS, D_W), jnp.float32) ** steps_of(key_list[7], (HS, D_W), ((0, 256),), -0.2, 0.2)), 0.01, 1.0),
        "master_routed": gaussian(key_list[8], (RH, D_W), 1.0, 6.0, ((0, 256),), jnp.float32),
        "moment_routed": gaussian(key_list[9], (RH, D_W), 0.3, 1.8, ((0, 256),), jnp.float32),
        "second_routed": jnp.clip(jnp.exp(math.log(1.0) - 4.6051702 * jax.random.uniform(key_list[10], (RH, D_W), jnp.float32) ** steps_of(key_list[10], (RH, D_W), ((0, 256),), -0.2, 0.2)), 0.01, 1.0),
    }


def adamw(grad, master, moment, second):
    corr_one = 1.0 - 0.9 ** 20
    corr_two = 1.0 - 0.95 ** 20
    new_moment = 0.9 * moment + 0.1 * grad
    new_second = 0.95 * second + 0.05 * grad * grad
    step_dir = new_moment / corr_one / (jnp.sqrt(new_second / corr_two) + 1e-08)
    new_master = master - 0.02 * (step_dir + 0.1 * master)
    return (new_moment, new_second, new_master.astype(jnp.bfloat16))

def reference(hid_shared, hid_routed, out_grad, slot_token, slot_count, master_shared, moment_shared, second_shared, master_routed, moment_routed, second_routed):
    grad_shared = jnp.dot(hid_shared.T, out_grad, preferred_element_type=jnp.float32)
    slot_index = jnp.arange(SLOTS, dtype=jnp.int32)
    owner = slot_index // CAP
    live = slot_index % CAP < slot_count[owner]
    token_index = (owner * TOK_DEV + slot_token).astype(jnp.int32)
    slot_grad = out_grad[token_index]
    live_act = jnp.where(live[:, None], hid_routed, jnp.zeros_like(hid_routed))
    grad_routed = jnp.dot(live_act.T, slot_grad, preferred_element_type=jnp.float32)
    moment_s, second_s, weight_s = adamw(grad_shared, master_shared, moment_shared, second_shared)
    moment_r, second_r, weight_r = adamw(grad_routed, master_routed, moment_routed, second_routed)
    return (moment_s, second_s, moment_r, second_r, weight_s, weight_r)
```

```python
import jax
import jax.numpy as jnp
import numpy as np
from jax import lax
from jax.sharding import Mesh, PartitionSpec as P

AXES = ("yh", "core", "yl", "z", "x")
NX, NY, NZ = 4, 4, 8
SCALE = 0.25
BF = jnp.bfloat16
F32 = jnp.float32
F16 = jnp.float16


def adamw(grad, master, moment, second):
    corr_one = 1.0 - 0.9**20
    corr_two = 1.0 - 0.95**20
    new_moment = 0.9 * moment + 0.1 * grad
    new_second = 0.95 * second + 0.05 * grad * grad
    step_dir = new_moment / corr_one / (jnp.sqrt(new_second / corr_two) + 1e-08)
    new_master = master - 0.02 * (step_dir + 0.1 * master)
    return (new_moment, new_second, new_master.astype(BF))


def x_ring(v, d):
    return lax.ppermute(v, "x", [(i, (i + d) % NX) for i in range(NX)])


def y_ring(v, d):
    return lax.ppermute(v, ("yh", "yl"), [(i, (i + d) % NY) for i in range(NY)])


def core_swap(v):
    return lax.ppermute(v, "core", [(0, 1), (1, 0)])


def row_order(sr, rr):
    rows = sr + rr
    n = NX * NY * NZ * rows
    xs, ys, zs, i = np.meshgrid(np.arange(NX), np.arange(NY), np.arange(NZ), np.arange(rows), indexing="ij")
    dev = ((ys % 2) * NZ + zs) * NX + xs
    shared = np.zeros((n, 2 * 2 * NZ * NX * sr), np.float32)
    flat = np.arange(n)
    col = ((ys // 2) * (2 * NZ * NX) + dev) * sr + i
    keep = (i < sr).reshape(-1)
    shared[flat[keep], col.reshape(-1)[keep]] = 1
    routed = []
    for core in range(2):
        one = np.zeros((n, 4 * 2 * NZ * NX * rr), np.float32)
        col = (((ys // 2) * 2 + core) * (2 * NZ * NX) + dev) * rr + i - sr
        one[flat[~keep], col.reshape(-1)[~keep]] = 1
        routed.append(one)
    return shared.astype(jnp.bfloat16), np.stack(routed).astype(jnp.bfloat16)


def dot_t(a, b):
    return lax.dot_general(a, b, (((1,), (1,)), ((), ())), preferred_element_type=F32)


def dot(a, b):
    return jnp.dot(a, b, preferred_element_type=F32)


def local(
    hid_shared,
    hid_routed,
    out_grad,
    slot_token,
    slot_count,
    master_shared,
    moment_shared,
    second_shared,
    master_routed,
    moment_routed,
    second_routed,
):
    tok, width = out_grad.shape
    slots = hid_routed.shape[0]
    sr, rr = master_shared.shape[0], master_routed.shape[0]
    rows = sr + rr
    half = width // 2
    cut = hid_shared.shape[1] // 4
    core = lax.axis_index("core")
    x = lax.axis_index("x")
    yh, yl = lax.axis_index("yh"), lax.axis_index("yl")
    y = yh * 2 + yl

    shared_order, routed_order = row_order(sr, rr)
    shared_order = jnp.asarray(shared_order)
    routed_order = jnp.asarray(routed_order)
    live = lax.iota(jnp.int32, slots) < slot_count[0]
    place = (slot_token[:, None] == lax.broadcasted_iota(jnp.int32, (slots, tok), 1)) & live[:, None]
    place = place.astype(BF)

    def activ(k):
        cols = [lax.dynamic_slice(hid_shared, (0, (h * 2 + k) * cut), (tok, cut)) for h in range(2)]
        one = dot_t(shared_order, jnp.concatenate(cols, axis=1))
        order = lax.dynamic_index_in_dim(routed_order, k, 0, keepdims=False)
        two = dot(dot_t(order, hid_routed).astype(BF), place)
        return (one + two).astype(BF)

    og = (out_grad[:, :half], out_grad[:, half:])
    og_far = [None, None]
    og_far[0] = core_swap(og[0])
    act_far = core_swap(activ(1 - core))
    og_far[1] = core_swap(og[1])
    act_near = activ(core)

    group = NZ * rows
    act_near = act_near.reshape(NX, NY, group, tok)
    act_far = act_far.reshape(NX, NY, group, tok)

    def term(part, dim, index):
        def pick(a):
            return lax.dynamic_index_in_dim(a, index, dim, keepdims=False).reshape(-1, tok)

        total = dot(pick(act_near), og[part]) + dot(pick(act_far), og_far[part])
        return SCALE * total

    rings = (x_ring, y_ring)
    place_of = (x, y)
    firsts = []
    for part in range(2):
        ring, me = rings[part], place_of[part]
        got = [ring(term(part, part, (me + d) % 4).astype(F16), d) for d in (2, 1, 3)]
        total = term(part, part, me)
        for g in got:
            total = total + g.astype(F32)
        firsts.append(total.reshape(4, group, half))
    seconds = []
    for part in range(2):
        ring, me = rings[1 - part], place_of[1 - part]

        def pick(index):
            return lax.dynamic_index_in_dim(firsts[part], index, 0, keepdims=False)

        got = [ring(pick((me + d) % 4).astype(F16), d) for d in (2, 1, 3)]
        total = pick(me)
        for g in got:
            total = total + g.astype(F32)
        seconds.append(total.astype(F16))
    last = jnp.concatenate(seconds, axis=1).reshape(NZ, rows * width // 128, 128)
    last = lax.all_to_all(last, "z", 0, 0)
    grad = (last.astype(F32).sum(axis=0) * (1.0 / SCALE)).reshape(rows, width)

    moment_s, second_s, weight_s = adamw(grad[:sr], master_shared, moment_shared, second_shared)
    moment_r, second_r, weight_r = adamw(grad[sr:], master_routed, moment_routed, second_routed)

    weight = jnp.concatenate([weight_s, weight_r], axis=0).reshape(rows * width // 128, 128)
    by_z = lax.all_gather(weight, "z", axis=0, tiled=False).reshape(NZ * rows, width)
    by_y = lax.ppermute(by_z, "yl", [(0, 1), (1, 0)])
    mine = jnp.concatenate([by_z, by_y], axis=0)
    full = jnp.concatenate([mine] + [x_ring(mine, d) for d in (1, 2, 3)], axis=0)

    def final(count, low, outer):
        r = lax.broadcasted_iota(jnp.int32, (outer, full.shape[0]), 0)
        q = lax.broadcasted_iota(jnp.int32, (outer, full.shape[0]), 1)
        i = r % count
        xx = (r // count) % NX
        zz = (r // (count * NX)) % NZ
        yy = r // (count * NX * NZ)
        back = (x - xx) % NX
        flip = yy ^ yl
        want = ((back * 2 + flip) * NZ + zz) * rows + low + i
        return dot((q == want).astype(BF), full).astype(BF)

    n = 2 * NZ * NX
    return (moment_s, second_s, moment_r, second_r, final(sr, 0, n * sr), final(rr, sr, n * rr))


def solution(mesh):
    fine = Mesh(mesh.devices.reshape(2, 2, 2, NZ, NX), AXES)
    split = P(AXES, None)
    flat = P(AXES)
    cuts = P(("yh", "core"), None)
    return jax.shard_map(
        local,
        mesh=fine,
        in_specs=(split, split, split, flat, flat) + (split,) * 6,
        out_specs=(split,) * 4 + (cuts,) * 2,
        check_vma=False,
    )
```

```python
import jax
import jax.numpy as jnp
import numpy as np
from jax import lax
from jax.experimental import pallas as pl
from jax.experimental.pallas import tpu as pltpu
from jax.sharding import Mesh, PartitionSpec as P

AXES = ("yh", "core", "yl", "z", "x")
NX, NY, NZ = 4, 4, 8
SCALE = 0.25
BF = jnp.bfloat16
F32 = jnp.float32
F16 = jnp.float16


def adamw(grad, master, moment, second):
    corr_one = 1.0 - 0.9**20
    corr_two = 1.0 - 0.95**20
    new_moment = 0.9 * moment + 0.1 * grad
    new_second = 0.95 * second + 0.05 * grad * grad
    step_dir = new_moment / corr_one / (jnp.sqrt(new_second / corr_two) + 1e-08)
    new_master = master - 0.02 * (step_dir + 0.1 * master)
    return (new_moment, new_second, new_master.astype(BF))


def x_ring(v, d):
    return lax.ppermute(v, "x", [(i, (i + d) % NX) for i in range(NX)])


def y_ring(v, d):
    return lax.ppermute(v, ("yh", "yl"), [(i, (i + d) % NY) for i in range(NY)])


def y_swap(v):
    return lax.ppermute(v, "yl", [(0, 1), (1, 0)])


def core_swap(v):
    return lax.ppermute(v, "core", [(0, 1), (1, 0)])


def row_order(sr, rr):
    rows = sr + rr
    n = NX * 2 * NZ * rows
    xs, ys, zs, i = np.meshgrid(np.arange(NX), np.arange(2), np.arange(NZ), np.arange(rows), indexing="ij")
    dev = (ys * NZ + zs) * NX + xs
    flat = np.arange(n)
    keep = (i < sr).reshape(-1)
    shared = np.zeros((n, 2 * NZ * NX * sr), np.float32)
    shared[flat[keep], (dev * sr + i).reshape(-1)[keep]] = 1
    routed = np.zeros((2, n, 2, 2 * NZ * NX * rr), np.float32)
    for core in range(2):
        routed[core, flat[~keep], core, (dev * rr + i - sr).reshape(-1)[~keep]] = 1
    return shared.astype(BF), routed.reshape(2, n, -1).astype(BF)


def dot_t(a, b):
    return lax.dot_general(a, b, (((1,), (1,)), ((), ())), preferred_element_type=F32)


def dot(a, b):
    return jnp.dot(a, b, preferred_element_type=F32)


def order_kernel(core_ref, shared_ref, routed_ref, shared_order_ref, routed_order_ref, place_ref, out_ref):
    slots = dot_t(routed_order_ref[0], routed_ref[...]).astype(BF)
    total = dot_t(shared_order_ref[...], shared_ref[...]) + dot(slots, place_ref[...])
    out_ref[...] = total.astype(BF).reshape(out_ref.shape)


def ordered(core, hid_shared, hid_routed, shared_order, routed_order, place):
    tok = hid_shared.shape[0]
    slots = hid_routed.shape[0]
    n, cut = shared_order.shape
    pair = routed_order.shape[2]
    return pl.pallas_call(
        order_kernel,
        grid_spec=pltpu.PrefetchScalarGridSpec(
            num_scalar_prefetch=1,
            grid=(2,),
            in_specs=[
                pl.BlockSpec((tok, cut), lambda h, c: (0, h * 2 + c[0])),
                pl.BlockSpec((slots, pair), lambda h, c: (0, h)),
                pl.BlockSpec((n, cut), lambda h, c: (0, 0)),
                pl.BlockSpec((1, n, pair), lambda h, c: (c[0], 0, 0)),
                pl.BlockSpec((slots, tok), lambda h, c: (0, 0)),
            ],
            out_specs=pl.BlockSpec((NX, 1, n // NX, tok), lambda h, c: (0, h, 0, 0)),
        ),
        out_shape=jax.ShapeDtypeStruct((NX, 2, n // NX, tok), BF),
        compiler_params=pltpu.CompilerParams(vmem_limit_bytes=32 * 2**20),
        cost_estimate=pl.CostEstimate(flops=4 * n * cut * tok, bytes_accessed=6 * n * tok, transcendentals=0),
    )(core.reshape(1), hid_shared, hid_routed, shared_order, routed_order, place)


def local(
    hid_shared,
    hid_routed,
    out_grad,
    slot_token,
    slot_count,
    master_shared,
    moment_shared,
    second_shared,
    master_routed,
    moment_routed,
    second_routed,
):
    tok, width = out_grad.shape
    slots = hid_routed.shape[0]
    sr, rr = master_shared.shape[0], master_routed.shape[0]
    rows = sr + rr
    half = width // 2
    group = NZ * rows
    core = lax.axis_index("core")
    x = lax.axis_index("x")
    yh, yl = lax.axis_index("yh"), lax.axis_index("yl")
    y = yh * 2 + yl

    shared_order, routed_order = (jnp.asarray(v) for v in row_order(sr, rr))
    live = lax.iota(jnp.int32, slots) < slot_count[0]
    place = (slot_token[:, None] == lax.broadcasted_iota(jnp.int32, (slots, tok), 1)) & live[:, None]
    place = place.astype(BF)

    def activ(k):
        return ordered(k, hid_shared, hid_routed, shared_order, routed_order, place)

    out_far = core_swap(out_grad)
    act_far = core_swap(activ(1 - core)).reshape(NX, NY, group, tok)
    act_near = activ(core).reshape(NX, NY, group, tok)

    def term(near, far, part, index):
        def pick(a):
            return lax.dynamic_index_in_dim(a, index, part, keepdims=False).reshape(-1, tok)

        cols = slice(part * half, (part + 1) * half)
        total = dot(pick(near), out_grad[:, cols]) + dot(pick(far), out_far[:, cols])
        return SCALE * total

    rings = (x_ring, y_ring)
    place_of = (x, y)
    got = ([], [])
    far = act_far
    for d in (2, 1, 3):
        for part in range(2):
            sent = term(act_near, far, part, (place_of[part] + d) % 4).astype(F16)
            got[part].append(rings[part](sent, d))
    firsts = []
    for part in range(2):
        total = term(act_near, far, part, place_of[part])
        for g in got[part]:
            total = total + g.astype(F32)
        firsts.append(total.reshape(4, group, half))
    seconds = []
    for part in range(2):
        ring, me = rings[1 - part], place_of[1 - part]

        def pick(index):
            return lax.dynamic_index_in_dim(firsts[part], index, 0, keepdims=False)

        back = [ring(pick((me + d) % 4).astype(F16), d) for d in (2, 1, 3)]
        total = pick(me)
        for g in back:
            total = total + g.astype(F32)
        seconds.append(total.astype(F16))
    last = jnp.concatenate(seconds, axis=1).reshape(NZ, rows * width // 128, 128)
    last = lax.all_to_all(last, "z", 0, 0)
    grad = (last.astype(F32).sum(axis=0) * (1.0 / SCALE)).reshape(rows, width)

    moment_s, second_s, weight_s = adamw(grad[:sr], master_shared, moment_shared, second_shared)
    moment_r, second_r, weight_r = adamw(grad[sr:], master_routed, moment_routed, second_routed)

    weight_s = weight_s.reshape(1, sr * width // 128, 128)
    s_all = lax.all_to_all(jnp.broadcast_to(weight_s, (NZ,) + weight_s.shape[1:]), "z", 0, 0)
    weight_r = weight_r.reshape(rr * width // 128, 128)
    r_all = jnp.concatenate([weight_r] + [x_ring(weight_r, d) for d in (1, 2, 3)], axis=0)
    s_all = s_all.reshape(NZ * sr, width)
    s_all = jnp.concatenate([s_all, y_swap(s_all)], axis=0)
    r_all = jnp.concatenate([r_all, y_swap(r_all)], axis=0).reshape(2 * NX * rr, width)
    s_all = jnp.concatenate([s_all] + [x_ring(s_all, d) for d in (1, 2, 3)], axis=0)
    r_all = lax.all_gather(r_all, "z", axis=0, tiled=True)

    def final(full, count, index):
        n = full.shape[0]
        r = lax.iota(jnp.int32, n)
        i = r % count
        back = (x - (r // count) % NX) % NX
        zz = (r // (count * NX)) % NZ
        flip = (r // (count * NX * NZ)) ^ yl
        want = lax.optimization_barrier(index(back, flip, zz) * count + i)
        take = want[:, None] == lax.broadcasted_iota(jnp.int32, (n, n), 1)
        return dot(take.astype(BF), full).astype(BF)

    shared = final(s_all, sr, lambda back, flip, zz: (back * 2 + flip) * NZ + zz)
    routed = final(r_all, rr, lambda back, flip, zz: (zz * 2 + flip) * NX + back)
    return (moment_s, second_s, moment_r, second_r, shared, routed)


def solution(mesh):
    fine = Mesh(mesh.devices.reshape(2, 2, 2, NZ, NX), AXES)
    split = P(AXES, None)
    flat = P(AXES)
    cuts = P(("yh", "core"), None)
    return jax.shard_map(
        local,
        mesh=fine,
        in_specs=(split, split, split, flat, flat) + (split,) * 6,
        out_specs=(split,) * 4 + (cuts,) * 2,
        check_vma=False,
    )
```

```python
import jax
import jax.numpy as jnp
import numpy as np
from jax import lax
from jax.experimental import pallas as pl
from jax.experimental.pallas import tpu as pltpu
from jax.sharding import Mesh, PartitionSpec as P

AXES = ("yh", "core", "yl", "z", "x")
NX, NY, NZ = 4, 4, 8
SCALE = 0.25
BF = jnp.bfloat16
F32 = jnp.float32
F16 = jnp.float16


def adamw(grad, master, moment, second):
    corr_one = 1.0 - 0.9**20
    corr_two = 1.0 - 0.95**20
    new_moment = 0.9 * moment + 0.1 * grad
    new_second = 0.95 * second + 0.05 * grad * grad
    step_dir = new_moment / corr_one / (jnp.sqrt(new_second / corr_two) + 1e-08)
    new_master = master - 0.02 * (step_dir + 0.1 * master)
    return (new_moment, new_second, new_master.astype(BF))


def x_ring(v, d):
    return lax.ppermute(v, "x", [(i, (i + d) % NX) for i in range(NX)])


def y_ring(v, d):
    return lax.ppermute(v, ("yh", "yl"), [(i, (i + d) % NY) for i in range(NY)])


def y_swap(v):
    return lax.ppermute(v, "yl", [(0, 1), (1, 0)])


def core_swap(v):
    return lax.ppermute(v, "core", [(0, 1), (1, 0)])


def row_order(sr, rr):
    rows = sr + rr
    n = NX * 2 * NZ * rows
    xs, ys, zs, i = np.meshgrid(np.arange(NX), np.arange(2), np.arange(NZ), np.arange(rows), indexing="ij")
    dev = (ys * NZ + zs) * NX + xs
    flat = np.arange(n)
    keep = (i < sr).reshape(-1)
    shared = np.zeros((n, 2 * NZ * NX * sr), np.float32)
    shared[flat[keep], (dev * sr + i).reshape(-1)[keep]] = 1
    routed = np.zeros((2, n, 2, 2 * NZ * NX * rr), np.float32)
    for core in range(2):
        routed[core, flat[~keep], core, (dev * rr + i - sr).reshape(-1)[~keep]] = 1
    return shared.astype(BF), routed.reshape(2, n, -1).astype(BF)


def dot_t(a, b):
    return lax.dot_general(a, b, (((1,), (1,)), ((), ())), preferred_element_type=F32)


def dot(a, b):
    return jnp.dot(a, b, preferred_element_type=F32)


def order_kernel(core_ref, count_ref, token_ref, shared_ref, routed_ref, shared_order_ref, routed_order_ref, out_ref):
    tok, slots = shared_ref.shape[0], routed_ref.shape[0]
    names = lax.broadcasted_iota(jnp.int32, (tok, slots), 0) == token_ref[...]
    live = lax.broadcasted_iota(jnp.int32, (tok, slots), 1) < count_ref[0]
    place = jnp.where(names & live, 1.0, 0.0).astype(BF)
    slot_rows = dot_t(routed_order_ref[0], routed_ref[...]).astype(BF)
    total = dot_t(shared_order_ref[...], shared_ref[...]) + dot_t(slot_rows, place)
    out_ref[...] = total.astype(BF).reshape(out_ref.shape)


def ordered(core, count, token, hid_shared, hid_routed, shared_order, routed_order):
    tok = hid_shared.shape[0]
    slots = hid_routed.shape[0]
    n, cut = shared_order.shape
    pair = routed_order.shape[2]
    return pl.pallas_call(
        order_kernel,
        grid_spec=pltpu.PrefetchScalarGridSpec(
            num_scalar_prefetch=2,
            grid=(2,),
            in_specs=[
                pl.BlockSpec((1, slots), lambda h, c, m: (0, 0)),
                pl.BlockSpec((tok, cut), lambda h, c, m: (0, h * 2 + c[0])),
                pl.BlockSpec((slots, pair), lambda h, c, m: (0, h)),
                pl.BlockSpec((n, cut), lambda h, c, m: (0, 0)),
                pl.BlockSpec((1, n, pair), lambda h, c, m: (c[0], 0, 0)),
            ],
            out_specs=pl.BlockSpec((NX, 1, n // NX, tok), lambda h, c, m: (0, h, 0, 0)),
        ),
        out_shape=jax.ShapeDtypeStruct((NX, 2, n // NX, tok), BF),
        compiler_params=pltpu.CompilerParams(vmem_limit_bytes=56 * 2**20),
        cost_estimate=pl.CostEstimate(flops=8 * n * cut * tok, bytes_accessed=6 * n * tok, transcendentals=0),
    )(core.reshape(1), count, token.reshape(1, slots), hid_shared, hid_routed, shared_order, routed_order)


def local(
    hid_shared,
    hid_routed,
    out_grad,
    slot_token,
    slot_count,
    master_shared,
    moment_shared,
    second_shared,
    master_routed,
    moment_routed,
    second_routed,
):
    tok, width = out_grad.shape
    slots = hid_routed.shape[0]
    sr, rr = master_shared.shape[0], master_routed.shape[0]
    rows = sr + rr
    half = width // 2
    group = NZ * rows
    core = lax.axis_index("core")
    x = lax.axis_index("x")
    yh, yl = lax.axis_index("yh"), lax.axis_index("yl")
    y = yh * 2 + yl

    shared_order, routed_order = (jnp.asarray(v) for v in row_order(sr, rr))
    def activ(k):
        rows_of = ordered(k, slot_count, slot_token, hid_shared, hid_routed, shared_order, routed_order)
        return rows_of.reshape(NX, NY, group, tok)

    out_far = core_swap(out_grad)
    act_far = core_swap(activ(1 - core))
    act_near = activ(core)
    rings = (x_ring, y_ring)
    place_of = (x, y)
    quarter = half // 2

    def term(near, far, part, step, piece):
        def pick(a):
            index = (place_of[part] + step) % 4
            return lax.dynamic_index_in_dim(a, index, part, keepdims=False).reshape(-1, tok)

        start = part * half + piece * quarter
        cols = slice(start, start + quarter)
        total = dot(pick(near), out_grad[:, cols]) + dot(pick(far), out_far[:, cols])
        return SCALE * total

    order = [(part, piece, d) for part in range(2) for piece, d in ((0, 1), (1, -1))]
    near, far = act_near, act_far
    sent = [term(near, far, part, 2, piece).astype(F16) for part, piece, _ in order]
    relayed = [rings[part](v, d) for v, (part, _, d) in zip(sent, order)]
    near = lax.optimization_barrier((near, *sent))[0]
    got = {}
    for k, (part, piece, d) in enumerate(order):
        v = term(near, far, part, d, 1 - piece).astype(F16)
        if k:
            v, relayed[k - 1] = lax.optimization_barrier((v, relayed[k - 1]))
        got[part, 1 - piece] = [rings[part](v, d)]
    for k, (part, piece, d) in enumerate(order):
        total = term(near, far, part, d, piece) + relayed[k].astype(F32)
        got[part, piece].append(rings[part](total.astype(F16), d))
    lasts = []
    for part in range(2):
        firsts = []
        for piece in range(2):
            total = term(near, far, part, 0, piece)
            for g in got[part, piece]:
                total = total + g.astype(F32)
            firsts.append(total.reshape(4, group, quarter))
        ring, me = rings[1 - part], place_of[1 - part]

        def pick(step):
            both = [lax.dynamic_index_in_dim(f, (me + step) % 4, 0, keepdims=False) for f in firsts]
            return jnp.concatenate(both, axis=1)

        back = [ring(pick(d).astype(F16), d) for d in (2, 1, 3)]
        total = pick(0)
        for g in back:
            total = total + g.astype(F32)
        last = total.astype(F16).reshape(NZ, rows * half // 128, 128)
        last = lax.all_to_all(last, "z", 0, 0)
        lasts.append((last.astype(F32).sum(axis=0) * (1.0 / SCALE)).reshape(rows, half))
    grad = jnp.concatenate(lasts, axis=1)

    moment_s, second_s, weight_s = adamw(grad[:sr], master_shared, moment_shared, second_shared)
    moment_r, second_r, weight_r = adamw(grad[sr:], master_routed, moment_routed, second_routed)

    def spread_z(w):
        return lax.all_to_all(jnp.broadcast_to(w, (NZ,) + w.shape[1:]), "z", 0, 0)

    s_all = spread_z(weight_s.reshape(1, sr * width // 128, 128))
    weight_r = weight_r.reshape(rr * width // 128, 128)
    r_all = jnp.concatenate([weight_r] + [x_ring(weight_r, d) for d in (1, 2, 3)], axis=0)
    r_all = jnp.concatenate([r_all, y_swap(r_all)], axis=0)
    r_all = spread_z(r_all[None]).reshape(NZ * 2 * NX * rr, width)
    s_all = s_all.reshape(NZ * sr, width)
    s_both = [s_all, y_swap(s_all)]
    s_all = jnp.concatenate(s_both + [x_ring(v, d) for d in (1, 2, 3) for v in s_both], axis=0)

    def final(full, count, index):
        n = full.shape[0]
        r = lax.iota(jnp.int32, n)
        i = r % count
        back = (x - (r // count) % NX) % NX
        zz = (r // (count * NX)) % NZ
        flip = (r // (count * NX * NZ)) ^ yl
        want = lax.optimization_barrier(index(back, flip, zz) * count + i)
        take = want[:, None] == lax.broadcasted_iota(jnp.int32, (n, n), 1)
        return dot(take.astype(BF), full).astype(BF)

    shared = final(s_all, sr, lambda back, flip, zz: (back * 2 + flip) * NZ + zz)
    routed = final(r_all, rr, lambda back, flip, zz: (zz * 2 + flip) * NX + back)
    return (moment_s, second_s, moment_r, second_r, shared, routed)


def solution(mesh):
    fine = Mesh(mesh.devices.reshape(2, 2, 2, NZ, NX), AXES)
    split = P(AXES, None)
    flat = P(AXES)
    cuts = P(("yh", "core"), None)
    return jax.shard_map(
        local,
        mesh=fine,
        in_specs=(split, split, split, flat, flat) + (split,) * 6,
        out_specs=(split,) * 4 + (cuts,) * 2,
        check_vma=False,
    )
```

```python
import jax
import jax.numpy as jnp
import numpy as np
from jax import lax
from jax.experimental import pallas as pl
from jax.experimental.pallas import tpu as pltpu
from jax.sharding import Mesh, PartitionSpec as P

AXES = ("yh", "core", "yl", "z", "x")
NX, NY, NZ = 4, 4, 8
SCALE = 0.25
BF = jnp.bfloat16
F32 = jnp.float32
F16 = jnp.float16


def adamw(grad, master, moment, second):
    corr_one = 1.0 - 0.9**20
    corr_two = 1.0 - 0.95**20
    new_moment = 0.9 * moment + 0.1 * grad
    new_second = 0.95 * second + 0.05 * grad * grad
    step_dir = new_moment / corr_one / (jnp.sqrt(new_second / corr_two) + 1e-08)
    new_master = master - 0.02 * (step_dir + 0.1 * master)
    return (new_moment, new_second, new_master.astype(BF))


def x_ring(v, d):
    return lax.ppermute(v, "x", [(i, (i + d) % NX) for i in range(NX)])


def y_ring(v, d):
    return lax.ppermute(v, ("yh", "yl"), [(i, (i + d) % NY) for i in range(NY)])


def y_swap(v):
    return lax.ppermute(v, "yl", [(0, 1), (1, 0)])


def core_swap(v):
    return lax.ppermute(v, "core", [(0, 1), (1, 0)])


def row_order(sr, rr):
    rows = sr + rr
    n = NX * 2 * NZ * rows
    xs, ys, zs, i = np.meshgrid(np.arange(NX), np.arange(2), np.arange(NZ), np.arange(rows), indexing="ij")
    dev = (ys * NZ + zs) * NX + xs
    flat = np.arange(n)
    keep = (i < sr).reshape(-1)
    shared = np.zeros((n, 2 * NZ * NX * sr), np.float32)
    shared[flat[keep], (dev * sr + i).reshape(-1)[keep]] = 1
    routed = np.zeros((2, n, 2, 2 * NZ * NX * rr), np.float32)
    for core in range(2):
        routed[core, flat[~keep], core, (dev * rr + i - sr).reshape(-1)[~keep]] = 1
    return shared.astype(BF), routed.reshape(2, n, -1).astype(BF)


def dot_t(a, b):
    return lax.dot_general(a, b, (((1,), (1,)), ((), ())), preferred_element_type=F32)


def dot(a, b):
    return jnp.dot(a, b, preferred_element_type=F32)


def order_kernel(core_ref, count_ref, token_ref, shared_ref, routed_ref, shared_order_ref, routed_order_ref, out_ref):
    tok, slots = shared_ref.shape[0], routed_ref.shape[0]
    names = lax.broadcasted_iota(jnp.int32, (tok, slots), 0) == token_ref[...]
    live = lax.broadcasted_iota(jnp.int32, (tok, slots), 1) < count_ref[0]
    place = jnp.where(names & live, 1.0, 0.0).astype(BF)
    slot_rows = dot_t(routed_order_ref[0], routed_ref[...]).astype(BF)
    total = dot_t(shared_order_ref[...], shared_ref[...]) + dot_t(slot_rows, place)
    out_ref[...] = total.astype(BF).reshape(out_ref.shape)


def ordered(core, count, token, hid_shared, hid_routed, shared_order, routed_order):
    tok = hid_shared.shape[0]
    slots = hid_routed.shape[0]
    n, cut = shared_order.shape
    pair = routed_order.shape[2]
    return pl.pallas_call(
        order_kernel,
        grid_spec=pltpu.PrefetchScalarGridSpec(
            num_scalar_prefetch=2,
            grid=(2,),
            in_specs=[
                pl.BlockSpec((1, slots), lambda h, c, m: (0, 0)),
                pl.BlockSpec((tok, cut), lambda h, c, m: (0, h * 2 + c[0])),
                pl.BlockSpec((slots, pair), lambda h, c, m: (0, h)),
                pl.BlockSpec((n, cut), lambda h, c, m: (0, 0)),
                pl.BlockSpec((1, n, pair), lambda h, c, m: (c[0], 0, 0)),
            ],
            out_specs=pl.BlockSpec((NX, 1, n // NX, tok), lambda h, c, m: (0, h, 0, 0)),
        ),
        out_shape=jax.ShapeDtypeStruct((NX, 2, n // NX, tok), BF),
        compiler_params=pltpu.CompilerParams(vmem_limit_bytes=56 * 2**20),
        cost_estimate=pl.CostEstimate(flops=8 * n * cut * tok, bytes_accessed=6 * n * tok, transcendentals=0),
    )(core.reshape(1), count, token.reshape(1, slots), hid_shared, hid_routed, shared_order, routed_order)


def local(
    hid_shared,
    hid_routed,
    out_grad,
    slot_token,
    slot_count,
    master_shared,
    moment_shared,
    second_shared,
    master_routed,
    moment_routed,
    second_routed,
):
    tok, width = out_grad.shape
    slots = hid_routed.shape[0]
    sr, rr = master_shared.shape[0], master_routed.shape[0]
    rows = sr + rr
    half = width // 2
    group = NZ * rows
    core = lax.axis_index("core")
    x = lax.axis_index("x")
    yh, yl = lax.axis_index("yh"), lax.axis_index("yl")
    y = yh * 2 + yl

    shared_order, routed_order = (jnp.asarray(v) for v in row_order(sr, rr))
    def activ(k):
        rows_of = ordered(k, slot_count, slot_token, hid_shared, hid_routed, shared_order, routed_order)
        return rows_of.reshape(NX, NY, group, tok)

    out_far = core_swap(out_grad)
    act_far = core_swap(activ(1 - core))
    act_near = activ(core)

    def first(part):
        def lined(v):
            return (v.swapaxes(0, 1) if part else v).reshape(-1, tok)

        cols = slice(part * half, (part + 1) * half)
        total = dot(lined(act_near), out_grad[:, cols]) + dot(lined(act_far), out_far[:, cols])
        return (SCALE * total).astype(F16).reshape(4, 4 * group, half)

    def reduce_x(v):
        return lax.all_to_all(v, "x", 0, 0).astype(F32).sum(axis=0).astype(F16)

    def reduce_y(v):
        def pick(step):
            return lax.dynamic_index_in_dim(v, (y + step) % NY, 0, keepdims=False)

        back = [y_ring(pick(d), d) for d in (2, 1, 3)]
        return sum((b.astype(F32) for b in back), pick(0).astype(F32)).astype(F16)

    one_a, one_b = reduce_x(first(0)), reduce_y(first(1))
    two = [reduce_y(one_a.reshape(NY, group, half)), reduce_x(one_b.reshape(NX, group, half))]
    last = jnp.concatenate(two, axis=1).reshape(NZ, rows * width // 128, 128)
    last = lax.all_to_all(last, "z", 0, 0)
    grad = (last.astype(F32).sum(axis=0) * (1.0 / SCALE)).reshape(rows, width)

    moment_s, second_s, weight_s = adamw(grad[:sr], master_shared, moment_shared, second_shared)
    moment_r, second_r, weight_r = adamw(grad[sr:], master_routed, moment_routed, second_routed)

    weight = jnp.concatenate([weight_s, weight_r], axis=0).reshape(1, rows * width // 128, 128)
    weight = lax.all_to_all(jnp.broadcast_to(weight, (NZ,) + weight.shape[1:]), "z", 0, 0)
    weight = weight.reshape(group, width)
    one_a, one_b = weight[:, :half], weight[:, half:]
    one_a = jnp.concatenate([one_a, y_swap(one_a)], axis=0)
    one_b = jnp.concatenate([one_b] + [x_ring(one_b, d) for d in (1, 2, 3)], axis=0)
    all_a = [one_a] + [x_ring(one_a, d) for d in (1, 2, 3)]
    all_b = [one_b, y_swap(one_b)]

    def want(count, low, index):
        r = lax.iota(jnp.int32, 2 * NZ * NX * count)
        back = (x - (r // count) % NX) % NX
        zz = (r // (count * NX)) % NZ
        flip = (r // (count * NX * NZ)) ^ yl
        return (index(back, flip) * NZ + zz) * rows + low + r % count

    def wanted(index, blocks):
        r = jnp.concatenate([want(sr, 0, index), want(rr, sr, index)])
        r = lax.optimization_barrier(r)
        n = r.shape[0]
        q = lax.broadcasted_iota(jnp.int32, (blocks, n, n // blocks), 0) * (n // blocks)
        q = q + lax.broadcasted_iota(jnp.int32, q.shape, 2)
        return (r[None, :, None] == q).astype(BF)

    take_a = wanted(lambda back, flip: back * 2 + flip, len(all_a))
    take_b = wanted(lambda back, flip: flip * NX + back, len(all_b))
    shared, routed = settled(take_a, take_b, all_a, all_b, 2 * NZ * NX * sr)
    return (moment_s, second_s, moment_r, second_r, shared, routed)


def settle_kernel(take_a, take_b, *refs):
    a, b, (shared, routed) = refs[:4], refs[4:6], refs[6:]
    split = shared.shape[0]

    def put(take, blocks):
        total = sum(dot(take[k], v[...]) for k, v in enumerate(blocks)).astype(BF)
        shared[...] = total[:split]
        routed[...] = total[split:]

    first = pl.program_id(0) < pl.num_programs(0) // 2

    @pl.when(first)
    def _():
        put(take_a, a)

    @pl.when(jnp.logical_not(first))
    def _():
        put(take_b, b)


def settled(take_a, take_b, all_a, all_b, split):
    n = take_a.shape[1]
    half = all_a[0].shape[1]
    tile = 256
    steps = half // tile

    def tiles(v, low):
        return pl.BlockSpec((v.shape[0], tile), lambda j: (0, jnp.clip(j - low, 0, steps - 1)))

    def whole(v):
        return pl.BlockSpec(v.shape, lambda j: (0, 0, 0))

    return pl.pallas_call(
        settle_kernel,
        grid=(2 * steps,),
        in_specs=[whole(take_a), whole(take_b)] + [tiles(v, 0) for v in all_a] + [tiles(v, steps) for v in all_b],
        out_specs=[pl.BlockSpec((split, tile), lambda j: (0, j)), pl.BlockSpec((n - split, tile), lambda j: (0, j))],
        out_shape=[jax.ShapeDtypeStruct((split, 2 * half), BF), jax.ShapeDtypeStruct((n - split, 2 * half), BF)],
        compiler_params=pltpu.CompilerParams(vmem_limit_bytes=32 * 2**20),
    )(take_a, take_b, *all_a, *all_b)


def solution(mesh):
    fine = Mesh(mesh.devices.reshape(2, 2, 2, NZ, NX), AXES)
    split = P(AXES, None)
    flat = P(AXES)
    cuts = P(("yh", "core"), None)
    return jax.shard_map(
        local,
        mesh=fine,
        in_specs=(split, split, split, flat, flat) + (split,) * 6,
        out_specs=(split,) * 4 + (cuts,) * 2,
        check_vma=False,
    )
```

```python
import jax
import jax.numpy as jnp
import numpy as np
from jax import lax
from jax.experimental import pallas as pl
from jax.experimental.pallas import tpu as pltpu
from jax.sharding import Mesh, PartitionSpec as P

AXES = ("yh", "core", "yl", "z", "x")
NX, NY, NZ = 4, 4, 8
SCALE = 0.25
BF = jnp.bfloat16
F32 = jnp.float32
F16 = jnp.float16


def adamw(grad, master, moment, second):
    corr_one = 1.0 - 0.9**20
    corr_two = 1.0 - 0.95**20
    new_moment = 0.9 * moment + 0.1 * grad
    new_second = 0.95 * second + 0.05 * grad * grad
    step_dir = new_moment / corr_one / (jnp.sqrt(new_second / corr_two) + 1e-08)
    new_master = master - 0.02 * (step_dir + 0.1 * master)
    return (new_moment, new_second, new_master.astype(BF))


def x_ring(v, d):
    return lax.ppermute(v, "x", [(i, (i + d) % NX) for i in range(NX)])


def y_ring(v, d):
    return lax.ppermute(v, ("yh", "yl"), [(i, (i + d) % NY) for i in range(NY)])


def y_swap(v):
    return lax.ppermute(v, "yl", [(0, 1), (1, 0)])


def core_swap(v):
    return lax.ppermute(v, "core", [(0, 1), (1, 0)])


def row_order(sr, rr):
    rows = sr + rr
    n = NX * 2 * NZ * rows
    xs, ys, zs, i = np.meshgrid(np.arange(NX), np.arange(2), np.arange(NZ), np.arange(rows), indexing="ij")
    dev = (ys * NZ + zs) * NX + xs
    flat = np.arange(n)
    keep = (i < sr).reshape(-1)
    shared = np.zeros((n, 2 * NZ * NX * sr), np.float32)
    shared[flat[keep], (dev * sr + i).reshape(-1)[keep]] = 1
    routed = np.zeros((2, n, 2, 2 * NZ * NX * rr), np.float32)
    for core in range(2):
        routed[core, flat[~keep], core, (dev * rr + i - sr).reshape(-1)[~keep]] = 1
    return shared.astype(BF), routed.reshape(2, n, -1).astype(BF)


def dot_t(a, b):
    return lax.dot_general(a, b, (((1,), (1,)), ((), ())), preferred_element_type=F32)


def dot(a, b):
    return jnp.dot(a, b, preferred_element_type=F32)


def order_kernel(core_ref, count_ref, token_ref, shared_ref, routed_ref, shared_order_ref, routed_order_ref, far_a, far_b, near_a, near_b):
    tok, slots = shared_ref.shape[0], routed_ref.shape[0]
    names = lax.broadcasted_iota(jnp.int32, (tok, slots), 0) == token_ref[...]
    live = lax.broadcasted_iota(jnp.int32, (tok, slots), 1) < count_ref[0]
    place = jnp.where(names & live, 1.0, 0.0).astype(BF)
    slot_rows = dot_t(routed_order_ref[0], routed_ref[...]).astype(BF)
    total = dot_t(shared_order_ref[...], shared_ref[...]) + dot_t(slot_rows, place)
    group = total.shape[0] // (2 * NX)

    def put(a, b):
        a[...] = total.astype(BF).reshape(a.shape)
        for xx in range(NX):
            for yy in range(2):
                start = (xx * 2 + yy) * group
                b[yy, xx] = total[start : start + group].astype(BF)

    @pl.when(pl.program_id(0) < 2)
    def _():
        put(far_a, far_b)

    @pl.when(pl.program_id(0) >= 2)
    def _():
        put(near_a, near_b)


def ordered(core, count, token, hid_shared, hid_routed, shared_order, routed_order):
    tok = hid_shared.shape[0]
    slots = hid_routed.shape[0]
    n, cut = shared_order.shape
    pair = routed_order.shape[2]
    group = n // (2 * NX)

    def who(j, c):
        return jnp.where(j < 2, 1 - c[0], c[0])

    def out(low):
        def at(j):
            return jnp.clip(j - low, 0, 1)

        return [
            pl.BlockSpec((NX, 1, n // NX, tok), lambda j, c, m: (0, at(j), 0, 0)),
            pl.BlockSpec((2, NX, group, tok), lambda j, c, m: (at(j), 0, 0, 0)),
        ]

    shapes = [
        jax.ShapeDtypeStruct((NX, 2, n // NX, tok), BF),
        jax.ShapeDtypeStruct((NY, NX, group, tok), BF),
    ]
    return pl.pallas_call(
        order_kernel,
        grid_spec=pltpu.PrefetchScalarGridSpec(
            num_scalar_prefetch=2,
            grid=(4,),
            in_specs=[
                pl.BlockSpec((1, slots), lambda j, c, m: (0, 0)),
                pl.BlockSpec((tok, cut), lambda j, c, m: (0, (j % 2) * 2 + who(j, c))),
                pl.BlockSpec((slots, pair), lambda j, c, m: (0, j % 2)),
                pl.BlockSpec((n, cut), lambda j, c, m: (0, 0)),
                pl.BlockSpec((1, n, pair), lambda j, c, m: (who(j, c), 0, 0)),
            ],
            out_specs=out(0) + out(2),
        ),
        out_shape=shapes + shapes,
        compiler_params=pltpu.CompilerParams(vmem_limit_bytes=56 * 2**20),
        cost_estimate=pl.CostEstimate(flops=16 * n * cut * tok, bytes_accessed=20 * n * tok, transcendentals=0),
    )(core.reshape(1), count, token.reshape(1, slots), hid_shared, hid_routed, shared_order, routed_order)


def product_kernel(near_ref, far_ref, out_near_ref, out_far_ref, total_ref):
    total_ref[...] = SCALE * (dot(near_ref[...], out_near_ref[...]) + dot(far_ref[...], out_far_ref[...]))


def product(near, far, out_near, out_far, low):
    n, tok = near.shape
    width = out_near.shape[1] - low
    tile = 256

    def whole(v):
        return pl.BlockSpec(v.shape, lambda j: (0, 0))

    cols = pl.BlockSpec((tok, tile), lambda j: (0, j + low // tile))
    return pl.pallas_call(
        product_kernel,
        grid=(width // tile,),
        in_specs=[whole(near), whole(far), cols, cols],
        out_specs=pl.BlockSpec((n, tile), lambda j: (0, j)),
        out_shape=jax.ShapeDtypeStruct((n, width), F32),
        compiler_params=pltpu.CompilerParams(vmem_limit_bytes=40 * 2**20),
        cost_estimate=pl.CostEstimate(flops=4 * n * tok * width, bytes_accessed=4 * n * (tok + width), transcendentals=0),
    )(near, far, out_near, out_far)


def local(
    hid_shared,
    hid_routed,
    out_grad,
    slot_token,
    slot_count,
    master_shared,
    moment_shared,
    second_shared,
    master_routed,
    moment_routed,
    second_routed,
):
    tok, width = out_grad.shape
    slots = hid_routed.shape[0]
    sr, rr = master_shared.shape[0], master_routed.shape[0]
    rows = sr + rr
    half = width // 2
    group = NZ * rows
    core = lax.axis_index("core")
    x = lax.axis_index("x")
    yh, yl = lax.axis_index("yh"), lax.axis_index("yl")
    y = yh * 2 + yl

    shared_order, routed_order = (jnp.asarray(v) for v in row_order(sr, rr))
    part_a = width * 3 // 5
    out_far = core_swap(out_grad)
    far_a, far_b, near_a, near_b = ordered(
        core, slot_count, slot_token, hid_shared, hid_routed, shared_order, routed_order
    )
    far_a, far_b = core_swap(far_a), core_swap(far_b)

    def flat(v):
        return v.reshape(-1, tok)

    total_a = dot(flat(near_a), out_grad[:, :part_a]) + dot(flat(far_a), out_far[:, :part_a])
    total_a = (SCALE * total_a).astype(F16)
    near_b, total_a = lax.optimization_barrier((near_b, total_a))
    total_b = product(flat(near_b), flat(far_b), out_grad, out_far, part_a)

    def reduce_x(v):
        return lax.all_to_all(v, "x", 0, 0).astype(F32).sum(axis=0)

    def reduce_y(v):
        def pick(step):
            return lax.dynamic_index_in_dim(v, (y + step) % NY, 0, keepdims=False)

        back = [y_ring(pick(d).astype(F16), d) for d in (2, 1, 3)]
        return sum((b.astype(F32) for b in back), pick(0).astype(F32))

    one_a = reduce_x(total_a.reshape(NX, NY * group, -1))
    one_b = reduce_y(total_b.reshape(NY, NX * group, -1)).astype(F16)
    two_a = reduce_y(one_a.reshape(NY, group, -1)).astype(F16)
    two_b = reduce_x(one_b.reshape(NX, group, -1)).astype(F16)
    two = [two_a, two_b]
    last = jnp.concatenate(two, axis=1).reshape(NZ, rows * width // 128, 128)
    last = lax.all_to_all(last, "z", 0, 0)
    grad = (last.astype(F32).sum(axis=0) * (1.0 / SCALE)).reshape(rows, width)

    moment_s, second_s, weight_s = adamw(grad[:sr], master_shared, moment_shared, second_shared)
    moment_r, second_r, weight_r = adamw(grad[sr:], master_routed, moment_routed, second_routed)

    weight = jnp.concatenate([weight_s, weight_r], axis=0).reshape(1, rows * width // 128, 128)
    weight = lax.all_to_all(jnp.broadcast_to(weight, (NZ,) + weight.shape[1:]), "z", 0, 0)
    weight = weight.reshape(group, width)
    one_a, one_b = weight[:, :half], weight[:, half:]
    one_a = jnp.concatenate([one_a, y_swap(one_a)], axis=0)
    one_b = jnp.concatenate([one_b] + [x_ring(one_b, d) for d in (1, 2, 3)], axis=0)
    all_a = [one_a] + [x_ring(one_a, d) for d in (1, 2, 3)]
    all_b = [one_b, y_swap(one_b)]

    def want(count, low, index):
        r = lax.iota(jnp.int32, 2 * NZ * NX * count)
        back = (x - (r // count) % NX) % NX
        zz = (r // (count * NX)) % NZ
        flip = (r // (count * NX * NZ)) ^ yl
        return (index(back, flip) * NZ + zz) * rows + low + r % count

    def wanted(index, blocks):
        r = jnp.concatenate([want(sr, 0, index), want(rr, sr, index)])
        r = lax.optimization_barrier(r)
        n = r.shape[0]
        q = lax.broadcasted_iota(jnp.int32, (blocks, n, n // blocks), 0) * (n // blocks)
        q = q + lax.broadcasted_iota(jnp.int32, q.shape, 2)
        return (r[None, :, None] == q).astype(BF)

    take_a = wanted(lambda back, flip: back * 2 + flip, len(all_a))
    take_b = wanted(lambda back, flip: flip * NX + back, len(all_b))
    shared, routed = settled(take_a, take_b, all_a, all_b, 2 * NZ * NX * sr)
    return (moment_s, second_s, moment_r, second_r, shared, routed)


def settle_kernel(take_a, take_b, *refs):
    a, b, (shared, routed) = refs[:4], refs[4:6], refs[6:]
    split = shared.shape[0]

    def put(take, blocks):
        total = sum(dot(take[k], v[...]) for k, v in enumerate(blocks)).astype(BF)
        shared[...] = total[:split]
        routed[...] = total[split:]

    first = pl.program_id(0) < pl.num_programs(0) // 2

    @pl.when(first)
    def _():
        put(take_a, a)

    @pl.when(jnp.logical_not(first))
    def _():
        put(take_b, b)


def settled(take_a, take_b, all_a, all_b, split):
    n = take_a.shape[1]
    half = all_a[0].shape[1]
    tile = half // 2
    steps = half // tile

    def tiles(v, low):
        return pl.BlockSpec((v.shape[0], tile), lambda j: (0, jnp.clip(j - low, 0, steps - 1)))

    def whole(v):
        return pl.BlockSpec(v.shape, lambda j: (0, 0, 0))

    return pl.pallas_call(
        settle_kernel,
        grid=(2 * steps,),
        in_specs=[whole(take_a), whole(take_b)] + [tiles(v, 0) for v in all_a] + [tiles(v, steps) for v in all_b],
        out_specs=[pl.BlockSpec((split, tile), lambda j: (0, j)), pl.BlockSpec((n - split, tile), lambda j: (0, j))],
        out_shape=[jax.ShapeDtypeStruct((split, 2 * half), BF), jax.ShapeDtypeStruct((n - split, 2 * half), BF)],
        compiler_params=pltpu.CompilerParams(vmem_limit_bytes=32 * 2**20),
    )(take_a, take_b, *all_a, *all_b)


def solution(mesh):
    fine = Mesh(mesh.devices.reshape(2, 2, 2, NZ, NX), AXES)
    split = P(AXES, None)
    flat = P(AXES)
    cuts = P(("yh", "core"), None)
    return jax.shard_map(
        local,
        mesh=fine,
        in_specs=(split, split, split, flat, flat) + (split,) * 6,
        out_specs=(split,) * 4 + (cuts,) * 2,
        check_vma=False,
    )
```

```python
import jax
import jax.numpy as jnp
import numpy as np
from jax import lax
from jax.experimental import pallas as pl
from jax.experimental.pallas import tpu as pltpu
from jax.sharding import Mesh, PartitionSpec as P

AXES = ("yh", "core", "yl", "z", "x")
NX, NY, NZ = 4, 4, 8
SCALE = 0.25
BF = jnp.bfloat16
F32 = jnp.float32
F16 = jnp.float16


def adamw(grad, master, moment, second):
    corr_one = 1.0 - 0.9**20
    corr_two = 1.0 - 0.95**20
    new_moment = 0.9 * moment + 0.1 * grad
    new_second = 0.95 * second + 0.05 * grad * grad
    step_dir = new_moment / corr_one / (jnp.sqrt(new_second / corr_two) + 1e-08)
    new_master = master - 0.02 * (step_dir + 0.1 * master)
    return (new_moment, new_second, new_master.astype(BF))


def x_ring(v, d):
    return lax.ppermute(v, "x", [(i, (i + d) % NX) for i in range(NX)])


def y_ring(v, d):
    return lax.ppermute(v, ("yh", "yl"), [(i, (i + d) % NY) for i in range(NY)])


def y_swap(v):
    return lax.ppermute(v, "yl", [(0, 1), (1, 0)])


def core_swap(v):
    return lax.ppermute(v, "core", [(0, 1), (1, 0)])


def row_order(sr, rr):
    rows = sr + rr
    n = NX * 2 * NZ * rows
    xs, ys, zs, i = np.meshgrid(np.arange(NX), np.arange(2), np.arange(NZ), np.arange(rows), indexing="ij")
    dev = (ys * NZ + zs) * NX + xs
    flat = np.arange(n)
    keep = (i < sr).reshape(-1)
    shared = np.zeros((n, 2 * NZ * NX * sr), np.float32)
    shared[flat[keep], (dev * sr + i).reshape(-1)[keep]] = 1
    routed = np.zeros((2, n, 2, 2 * NZ * NX * rr), np.float32)
    for core in range(2):
        routed[core, flat[~keep], core, (dev * rr + i - sr).reshape(-1)[~keep]] = 1
    return shared.astype(BF), routed.reshape(2, n, -1).astype(BF)


def dot_t(a, b):
    return lax.dot_general(a, b, (((1,), (1,)), ((), ())), preferred_element_type=F32)


def dot(a, b):
    return jnp.dot(a, b, preferred_element_type=F32)


def order_kernel(core_ref, count_ref, token_ref, shared_ref, routed_ref, shared_order_ref, routed_order_ref, far, near):
    tok, slots = shared_ref.shape[0], routed_ref.shape[0]
    names = lax.broadcasted_iota(jnp.int32, (tok, slots), 0) == token_ref[...]
    live = lax.broadcasted_iota(jnp.int32, (tok, slots), 1) < count_ref[0]
    place = jnp.where(names & live, 1.0, 0.0).astype(BF)
    slot_rows = dot_t(routed_order_ref[0], routed_ref[...]).astype(BF)
    total = dot_t(shared_order_ref[...], shared_ref[...]) + dot_t(slot_rows, place)

    @pl.when(pl.program_id(0) < 2)
    def _():
        far[...] = total.astype(BF).reshape(far.shape)

    @pl.when(pl.program_id(0) >= 2)
    def _():
        near[...] = total.astype(BF).reshape(near.shape)


def ordered(core, count, token, hid_shared, hid_routed, shared_order, routed_order):
    tok = hid_shared.shape[0]
    slots = hid_routed.shape[0]
    n, cut = shared_order.shape
    pair = routed_order.shape[2]

    def who(j, c):
        return jnp.where(j < 2, 1 - c[0], c[0])

    def out(low):
        return pl.BlockSpec((NX, 1, n // NX, tok), lambda j, c, m: (0, jnp.clip(j - low, 0, 1), 0, 0))

    shape = jax.ShapeDtypeStruct((NX, 2, n // NX, tok), BF)
    return pl.pallas_call(
        order_kernel,
        grid_spec=pltpu.PrefetchScalarGridSpec(
            num_scalar_prefetch=2,
            grid=(4,),
            in_specs=[
                pl.BlockSpec((1, slots), lambda j, c, m: (0, 0)),
                pl.BlockSpec((tok, cut), lambda j, c, m: (0, (j % 2) * 2 + who(j, c))),
                pl.BlockSpec((slots, pair), lambda j, c, m: (0, j % 2)),
                pl.BlockSpec((n, cut), lambda j, c, m: (0, 0)),
                pl.BlockSpec((1, n, pair), lambda j, c, m: (who(j, c), 0, 0)),
            ],
            out_specs=[out(0), out(2)],
        ),
        out_shape=[shape, shape],
        compiler_params=pltpu.CompilerParams(vmem_limit_bytes=56 * 2**20),
        cost_estimate=pl.CostEstimate(flops=16 * n * cut * tok, bytes_accessed=20 * n * tok, transcendentals=0),
    )(core.reshape(1), count, token.reshape(1, slots), hid_shared, hid_routed, shared_order, routed_order)


def local(
    hid_shared,
    hid_routed,
    out_grad,
    slot_token,
    slot_count,
    master_shared,
    moment_shared,
    second_shared,
    master_routed,
    moment_routed,
    second_routed,
):
    tok, width = out_grad.shape
    slots = hid_routed.shape[0]
    sr, rr = master_shared.shape[0], master_routed.shape[0]
    rows = sr + rr
    group = NZ * rows
    core = lax.axis_index("core")
    x = lax.axis_index("x")
    yh, yl = lax.axis_index("yh"), lax.axis_index("yl")
    y = yh * 2 + yl

    shared_order, routed_order = (jnp.asarray(v) for v in row_order(sr, rr))
    part_a = width * 3 // 5
    out_far = core_swap(out_grad)
    far, near = ordered(core, slot_count, slot_token, hid_shared, hid_routed, shared_order, routed_order)
    far = core_swap(far).reshape(-1, tok)
    near = near.reshape(-1, tok)

    def term(near, cols):
        total = dot(near, out_grad[:, cols]) + dot(far, out_far[:, cols])
        return (SCALE * total).astype(F16).reshape(NX, NY, group, -1)

    def pick(v, dim, step):
        index = ((x, y)[dim] + step) % 4
        return lax.dynamic_index_in_dim(v, index, dim, keepdims=False)

    def cut(v, dim):
        return [pick(v, dim, d).astype(F16) for d in (2, 1, 3)]

    def send(chunks, dim):
        return [(x_ring, y_ring)[dim](v, d) for v, d in zip(chunks, (2, 1, 3))]

    def gathered(v, dim, back):
        return sum((b.astype(F32) for b in back), pick(v, dim, 0).astype(F32))

    total_a = term(near, slice(0, part_a))
    near, total_a = lax.optimization_barrier((near, total_a))
    total_b = term(near, slice(part_a, width))
    back_a = send(cut(total_a, 0), 0)
    back_b = send(cut(total_b, 1), 1)
    one_a = gathered(total_a, 0, back_a)[None]
    chunks_a = cut(one_a, 1)
    back_b[0], *chunks_a = lax.optimization_barrier((back_b[0], *chunks_a))
    two_a = send(chunks_a, 1)
    one_b = gathered(total_b, 1, back_b)[:, None]
    two_b = send(cut(one_b, 0), 0)
    two_a = gathered(one_a, 1, two_a)[0].astype(F16)
    two_a, *two_b = lax.optimization_barrier((two_a, *two_b))
    two_b = gathered(one_b, 0, two_b)[0].astype(F16)
    two = [two_a, two_b]
    last = jnp.concatenate(two, axis=1).reshape(NZ, rows * width // 128, 128)
    last = lax.all_to_all(last, "z", 0, 0)
    grad = (last.astype(F32).sum(axis=0) * (1.0 / SCALE)).reshape(rows, width)

    moment_s, second_s, weight_s = adamw(grad[:sr], master_shared, moment_shared, second_shared)
    moment_r, second_r, weight_r = adamw(grad[sr:], master_routed, moment_routed, second_routed)

    weight = jnp.concatenate([weight_s, weight_r], axis=0).reshape(1, rows * width // 128, 128)
    weight = lax.all_to_all(jnp.broadcast_to(weight, (NZ,) + weight.shape[1:]), "z", 0, 0)
    weight_s = weight[:, : sr * width // 128].reshape(NZ * sr, width)
    weight_r = weight[:, sr * width // 128 :].reshape(NZ * rr, width)
    all_s = jnp.concatenate([weight_s, y_swap(weight_s)], axis=0)
    all_r = jnp.concatenate([weight_r] + [x_ring(weight_r, d) for d in (1, 2, 3)], axis=0)
    all_s = jnp.concatenate([all_s] + [x_ring(all_s, d) for d in (1, 2, 3)], axis=0)
    all_r = jnp.concatenate([all_r, y_swap(all_r)], axis=0)

    def settled(full, count, index):
        n = full.shape[0]
        r = lax.iota(jnp.int32, n)
        back = (x - (r // count) % NX) % NX
        zz = (r // (count * NX)) % NZ
        flip = (r // (count * NX * NZ)) ^ yl
        want = lax.optimization_barrier((index(back, flip) * NZ + zz) * count + r % count)
        take = (want[:, None] == lax.broadcasted_iota(jnp.int32, (n, n), 1)).astype(BF)
        return dot(lax.optimization_barrier(take), full).astype(BF)

    shared = settled(all_s, sr, lambda back, flip: back * 2 + flip)
    routed = settled(all_r, rr, lambda back, flip: flip * NX + back)
    return (moment_s, second_s, moment_r, second_r, shared, routed)


def solution(mesh):
    fine = Mesh(mesh.devices.reshape(2, 2, 2, NZ, NX), AXES)
    split = P(AXES, None)
    flat = P(AXES)
    cuts = P(("yh", "core"), None)
    return jax.shard_map(
        local,
        mesh=fine,
        in_specs=(split, split, split, flat, flat) + (split,) * 6,
        out_specs=(split,) * 4 + (cuts,) * 2,
        check_vma=False,
    )
```

```python
import jax
import jax.numpy as jnp
import numpy as np
from jax import lax
from jax.experimental import pallas as pl
from jax.experimental.pallas import tpu as pltpu
from jax.sharding import Mesh, PartitionSpec as P

AXES = ("yh", "core", "yl", "z", "x")
NX, NY, NZ = 4, 4, 8
SCALE = 0.25
BF = jnp.bfloat16
F32 = jnp.float32
F16 = jnp.float16


def adamw(grad, master, moment, second):
    corr_one = 1.0 - 0.9**20
    corr_two = 1.0 - 0.95**20
    new_moment = 0.9 * moment + 0.1 * grad
    new_second = 0.95 * second + 0.05 * grad * grad
    step_dir = new_moment / corr_one / (jnp.sqrt(new_second / corr_two) + 1e-08)
    new_master = master - 0.02 * (step_dir + 0.1 * master)
    return (new_moment, new_second, new_master.astype(BF))


def x_ring(v, d):
    return lax.ppermute(v, "x", [(i, (i + d) % NX) for i in range(NX)])


def y_ring(v, d):
    return lax.ppermute(v, ("yh", "yl"), [(i, (i + d) % NY) for i in range(NY)])


def y_swap(v):
    return lax.ppermute(v, "yl", [(0, 1), (1, 0)])


def core_swap(v):
    return lax.ppermute(v, "core", [(0, 1), (1, 0)])


def after(done, v):
    return lax.optimization_barrier((v, *done))[0]


def row_order(sr, rr):
    rows = sr + rr
    n = NX * 2 * NZ * rows
    xs, ys, zs, i = np.meshgrid(np.arange(NX), np.arange(2), np.arange(NZ), np.arange(rows), indexing="ij")
    dev = (ys * NZ + zs) * NX + xs
    flat = np.arange(n)
    keep = (i < sr).reshape(-1)
    shared = np.zeros((n, 2 * NZ * NX * sr), np.float32)
    shared[flat[keep], (dev * sr + i).reshape(-1)[keep]] = 1
    routed = np.zeros((2, n, 2, 2 * NZ * NX * rr), np.float32)
    for core in range(2):
        routed[core, flat[~keep], core, (dev * rr + i - sr).reshape(-1)[~keep]] = 1
    return shared.astype(BF), routed.reshape(2, n, -1).astype(BF)


def dot_t(a, b):
    return lax.dot_general(a, b, (((1,), (1,)), ((), ())), preferred_element_type=F32)


def dot(a, b):
    return jnp.dot(a, b, preferred_element_type=F32)


def order_kernel(core_ref, count_ref, token_ref, shared_ref, routed_ref, shared_order_ref, routed_order_ref, far, near):
    tok, slots = shared_ref.shape[0], routed_ref.shape[0]
    names = lax.broadcasted_iota(jnp.int32, (tok, slots), 0) == token_ref[...]
    live = lax.broadcasted_iota(jnp.int32, (tok, slots), 1) < count_ref[0]
    place = jnp.where(names & live, 1.0, 0.0).astype(BF)
    slot_rows = dot_t(routed_order_ref[0], routed_ref[...]).astype(BF)
    total = dot_t(shared_order_ref[...], shared_ref[...]) + dot_t(slot_rows, place)

    @pl.when(pl.program_id(0) < 2)
    def _():
        far[...] = total.astype(BF).reshape(far.shape)

    @pl.when(pl.program_id(0) >= 2)
    def _():
        near[...] = total.astype(BF).reshape(near.shape)


def ordered(core, count, token, hid_shared, hid_routed, shared_order, routed_order):
    tok = hid_shared.shape[0]
    slots = hid_routed.shape[0]
    n, cut = shared_order.shape
    pair = routed_order.shape[2]

    def who(j, c):
        return jnp.where(j < 2, 1 - c[0], c[0])

    def out(low):
        return pl.BlockSpec((NX, 1, n // NX, tok), lambda j, c, m: (0, jnp.clip(j - low, 0, 1), 0, 0))

    shape = jax.ShapeDtypeStruct((NX, 2, n // NX, tok), BF)
    return pl.pallas_call(
        order_kernel,
        grid_spec=pltpu.PrefetchScalarGridSpec(
            num_scalar_prefetch=2,
            grid=(4,),
            in_specs=[
                pl.BlockSpec((1, slots), lambda j, c, m: (0, 0)),
                pl.BlockSpec((tok, cut), lambda j, c, m: (0, (j % 2) * 2 + who(j, c))),
                pl.BlockSpec((slots, pair), lambda j, c, m: (0, j % 2)),
                pl.BlockSpec((n, cut), lambda j, c, m: (0, 0)),
                pl.BlockSpec((1, n, pair), lambda j, c, m: (who(j, c), 0, 0)),
            ],
            out_specs=[out(0), out(2)],
        ),
        out_shape=[shape, shape],
        compiler_params=pltpu.CompilerParams(vmem_limit_bytes=56 * 2**20),
        cost_estimate=pl.CostEstimate(flops=16 * n * cut * tok, bytes_accessed=20 * n * tok, transcendentals=0),
    )(core.reshape(1), count, token.reshape(1, slots), hid_shared, hid_routed, shared_order, routed_order)


def local(
    hid_shared,
    hid_routed,
    out_grad,
    slot_token,
    slot_count,
    master_shared,
    moment_shared,
    second_shared,
    master_routed,
    moment_routed,
    second_routed,
):
    tok, width = out_grad.shape
    slots = hid_routed.shape[0]
    sr, rr = master_shared.shape[0], master_routed.shape[0]
    rows = sr + rr
    group = NZ * rows
    core = lax.axis_index("core")
    x = lax.axis_index("x")
    yh, yl = lax.axis_index("yh"), lax.axis_index("yl")
    y = yh * 2 + yl

    shared_order, routed_order = (jnp.asarray(v) for v in row_order(sr, rr))
    part_a = width * 3 // 5
    out_far = core_swap(out_grad)
    far, near = ordered(core, slot_count, slot_token, hid_shared, hid_routed, shared_order, routed_order)
    far = core_swap(far).reshape(-1, tok)
    near = near.reshape(-1, tok)

    def term(near, cols):
        total = dot(near, out_grad[:, cols]) + dot(far, out_far[:, cols])
        return (SCALE * total).astype(F16).reshape(NX, NY, group, -1)

    def pick(v, dim, step):
        index = ((x, y)[dim] + step) % 4
        return lax.dynamic_index_in_dim(v, index, dim, keepdims=False)

    def cut(v, dim):
        return [pick(v, dim, d).astype(F16) for d in (2, 1, 3)]

    def send(chunks, dim):
        return [(x_ring, y_ring)[dim](v, d) for v, d in zip(chunks, (2, 1, 3))]

    def gathered(v, dim, back):
        return sum((b.astype(F32) for b in back), pick(v, dim, 0).astype(F32))

    def halves(total, dim):
        two, ahead, behind = (pick(total, dim, d) for d in (2, 1, 3))
        plus = jnp.concatenate([two[:2], ahead[2:]])
        minus = jnp.concatenate([two[2:], behind[:2]])
        return plus, minus

    def both(chunks, dim):
        ring = (x_ring, y_ring)[dim]
        return ring(chunks[0], 1), ring(chunks[1], 3)

    def relayed(total, dim, plus, minus):
        ahead = pick(total, dim, 1)[:2].astype(F32) + plus[:2].astype(F32)
        behind = pick(total, dim, 3)[2:].astype(F32) + minus[:2].astype(F32)
        return both((ahead.astype(F16), behind.astype(F16)), dim)

    def summed(total, dim, plus, minus, ahead, behind):
        got = jnp.concatenate([minus[2:], plus[2:]]).astype(F32)
        got = got + jnp.concatenate([ahead, behind]).astype(F32)
        return pick(total, dim, 0).astype(F32) + got

    total_a = term(near, slice(0, part_a))
    first_a = halves(total_a, 0)
    near = after(first_a, near)
    total_b = term(near, slice(part_a, width))
    first_a = both(first_a, 0)
    first_b = both(halves(total_b, 1), 1)
    one_a = summed(total_a, 0, *first_a, *relayed(total_a, 0, *first_a))[None]
    last_b = relayed(total_b, 1, *first_b)
    chunks_a = cut(one_a, 1)
    last_b = [after(chunks_a, v) for v in last_b]
    two_a = send(chunks_a, 1)
    one_b = summed(total_b, 1, *first_b, *last_b)[:, None]
    two_b = send(cut(one_b, 0), 0)
    two_a = gathered(one_a, 1, two_a)[0].astype(F16)
    two_b = [after([two_a], v) for v in two_b]
    two_b = gathered(one_b, 0, two_b)[0].astype(F16)
    two = [two_a, two_b]
    last = jnp.concatenate(two, axis=1).reshape(NZ, rows * width // 128, 128)
    last = lax.all_to_all(last, "z", 0, 0)
    grad = (last.astype(F32).sum(axis=0) * (1.0 / SCALE)).reshape(rows, width)

    moment_s, second_s, weight_s = adamw(grad[:sr], master_shared, moment_shared, second_shared)
    moment_r, second_r, weight_r = adamw(grad[sr:], master_routed, moment_routed, second_routed)

    weight = jnp.concatenate([weight_s, weight_r], axis=0).reshape(1, rows * width // 128, 128)
    weight = lax.all_to_all(jnp.broadcast_to(weight, (NZ,) + weight.shape[1:]), "z", 0, 0)
    weight_s = weight[:, : sr * width // 128].reshape(NZ * sr, width)
    weight_r = weight[:, sr * width // 128 :].reshape(NZ * rr, width)
    all_s = jnp.concatenate([weight_s, y_swap(weight_s)], axis=0)
    all_r = jnp.concatenate([weight_r] + [x_ring(weight_r, d) for d in (1, 2, 3)], axis=0)
    one_way, other_way = x_ring(all_s, 1), x_ring(all_s, 3)
    split = all_s.shape[0] // 2
    two_away = [x_ring(one_way[:split], 1), x_ring(other_way[split:], 3)]
    all_s = jnp.concatenate([all_s, one_way] + two_away + [other_way], axis=0)
    all_r = jnp.concatenate([all_r, y_swap(all_r)], axis=0)

    def settled(full, count, index):
        n = full.shape[0]
        r = lax.iota(jnp.int32, n)
        back = (x - (r // count) % NX) % NX
        zz = (r // (count * NX)) % NZ
        flip = (r // (count * NX * NZ)) ^ yl
        want = lax.optimization_barrier((index(back, flip) * NZ + zz) * count + r % count)
        take = (want[:, None] == lax.broadcasted_iota(jnp.int32, (n, n), 1)).astype(BF)
        return dot(lax.optimization_barrier(take), full).astype(BF)

    shared = settled(all_s, sr, lambda back, flip: back * 2 + flip)
    routed = settled(all_r, rr, lambda back, flip: flip * NX + back)
    return (moment_s, second_s, moment_r, second_r, shared, routed)


def solution(mesh):
    fine = Mesh(mesh.devices.reshape(2, 2, 2, NZ, NX), AXES)
    split = P(AXES, None)
    flat = P(AXES)
    cuts = P(("yh", "core"), None)
    return jax.shard_map(
        local,
        mesh=fine,
        in_specs=(split, split, split, flat, flat) + (split,) * 6,
        out_specs=(split,) * 4 + (cuts,) * 2,
        check_vma=False,
    )
```

```python
import jax
import jax.numpy as jnp
import numpy as np
from jax import lax
from jax.experimental import pallas as pl
from jax.experimental.pallas import tpu as pltpu
from jax.sharding import Mesh, PartitionSpec as P

AXES = ("yh", "core", "yl", "z", "x")
NX, NY, NZ = 4, 4, 8
SCALE = 0.25
BF = jnp.bfloat16
F32 = jnp.float32
F16 = jnp.float16


def adamw(grad, master, moment, second):
    corr_one = 1.0 - 0.9**20
    corr_two = 1.0 - 0.95**20
    new_moment = 0.9 * moment + 0.1 * grad
    new_second = 0.95 * second + 0.05 * grad * grad
    step_dir = new_moment / corr_one / (jnp.sqrt(new_second / corr_two) + 1e-08)
    new_master = master - 0.02 * (step_dir + 0.1 * master)
    return (new_moment, new_second, new_master.astype(BF))


def x_ring(v, d):
    return lax.ppermute(v, "x", [(i, (i + d) % NX) for i in range(NX)])


def y_ring(v, d):
    return lax.ppermute(v, ("yh", "yl"), [(i, (i + d) % NY) for i in range(NY)])


def y_swap(v):
    return lax.ppermute(v, "yl", [(0, 1), (1, 0)])


def core_swap(v):
    return lax.ppermute(v, "core", [(0, 1), (1, 0)])


def after(done, v):
    return lax.optimization_barrier((v, *done))[0]


def row_order(sr, rr):
    rows = sr + rr
    n = NX * 2 * NZ * rows
    xs, ys, zs, i = np.meshgrid(np.arange(NX), np.arange(2), np.arange(NZ), np.arange(rows), indexing="ij")
    dev = (ys * NZ + zs) * NX + xs
    flat = np.arange(n)
    keep = (i < sr).reshape(-1)
    shared = np.zeros((n, 2 * NZ * NX * sr), np.float32)
    shared[flat[keep], (dev * sr + i).reshape(-1)[keep]] = 1
    routed = np.zeros((2, n, 2, 2 * NZ * NX * rr), np.float32)
    for core in range(2):
        routed[core, flat[~keep], core, (dev * rr + i - sr).reshape(-1)[~keep]] = 1
    return shared.astype(BF), routed.reshape(2, n, -1).astype(BF)


def dot_t(a, b):
    return lax.dot_general(a, b, (((1,), (1,)), ((), ())), preferred_element_type=F32)


def dot(a, b):
    return jnp.dot(a, b, preferred_element_type=F32)


def order_kernel(core_ref, count_ref, token_ref, shared_ref, routed_ref, shared_order_ref, routed_order_ref, far, near):
    tok, slots = shared_ref.shape[0], routed_ref.shape[0]
    names = lax.broadcasted_iota(jnp.int32, (tok, slots), 0) == token_ref[...]
    live = lax.broadcasted_iota(jnp.int32, (tok, slots), 1) < count_ref[0]
    place = jnp.where(names & live, 1.0, 0.0).astype(BF)
    slot_rows = dot_t(routed_order_ref[0], routed_ref[...]).astype(BF)
    order = jnp.concatenate([shared_order_ref[...], slot_rows], axis=1)
    total = dot_t(order, jnp.concatenate([shared_ref[...], place], axis=1))

    @pl.when(pl.program_id(0) < 2)
    def _():
        far[...] = total.astype(BF).reshape(far.shape)

    @pl.when(pl.program_id(0) >= 2)
    def _():
        near[...] = total.astype(BF).reshape(near.shape)


def ordered(core, count, token, hid_shared, hid_routed, shared_order, routed_order):
    tok = hid_shared.shape[0]
    slots = hid_routed.shape[0]
    n, cut = shared_order.shape
    pair = routed_order.shape[2]

    def who(j, c):
        return jnp.where(j < 2, 1 - c[0], c[0])

    def out(low):
        return pl.BlockSpec((NX, 1, n // NX, tok), lambda j, c, m: (0, jnp.clip(j - low, 0, 1), 0, 0))

    shape = jax.ShapeDtypeStruct((NX, 2, n // NX, tok), BF)
    return pl.pallas_call(
        order_kernel,
        grid_spec=pltpu.PrefetchScalarGridSpec(
            num_scalar_prefetch=2,
            grid=(4,),
            in_specs=[
                pl.BlockSpec((1, slots), lambda j, c, m: (0, 0)),
                pl.BlockSpec((tok, cut), lambda j, c, m: (0, (j % 2) * 2 + who(j, c))),
                pl.BlockSpec((slots, pair), lambda j, c, m: (0, j % 2)),
                pl.BlockSpec((n, cut), lambda j, c, m: (0, 0)),
                pl.BlockSpec((1, n, pair), lambda j, c, m: (who(j, c), 0, 0)),
            ],
            out_specs=[out(0), out(2)],
        ),
        out_shape=[shape, shape],
        compiler_params=pltpu.CompilerParams(vmem_limit_bytes=56 * 2**20),
        cost_estimate=pl.CostEstimate(flops=16 * n * cut * tok, bytes_accessed=20 * n * tok, transcendentals=0),
    )(core.reshape(1), count, token.reshape(1, slots), hid_shared, hid_routed, shared_order, routed_order)


def local(
    hid_shared,
    hid_routed,
    out_grad,
    slot_token,
    slot_count,
    master_shared,
    moment_shared,
    second_shared,
    master_routed,
    moment_routed,
    second_routed,
):
    tok, width = out_grad.shape
    slots = hid_routed.shape[0]
    sr, rr = master_shared.shape[0], master_routed.shape[0]
    rows = sr + rr
    group = NZ * rows
    core = lax.axis_index("core")
    x = lax.axis_index("x")
    yh, yl = lax.axis_index("yh"), lax.axis_index("yl")
    y = yh * 2 + yl

    shared_order, routed_order = (jnp.asarray(v) for v in row_order(sr, rr))
    part_a = width * 3 // 5
    out_far = core_swap(out_grad)
    far, near = ordered(core, slot_count, slot_token, hid_shared, hid_routed, shared_order, routed_order)
    far = core_swap(far).reshape(-1, tok)
    near = near.reshape(-1, tok)

    def term(near, cols):
        total = dot(near, out_grad[:, cols]) + dot(far, out_far[:, cols])
        return (SCALE * total).astype(F16).reshape(NX, NY, group, -1)

    def pick(v, dim, step):
        index = ((x, y)[dim] + step) % 4
        return lax.dynamic_index_in_dim(v, index, dim, keepdims=False)

    def cut(v, dim):
        return [pick(v, dim, d).astype(F16) for d in (2, 1, 3)]

    def send(chunks, dim):
        return [(x_ring, y_ring)[dim](v, d) for v, d in zip(chunks, (2, 1, 3))]

    def gathered(v, dim, back):
        return sum((b.astype(F32) for b in back), pick(v, dim, 0).astype(F32))

    def front(v):
        return lax.broadcasted_iota(jnp.int32, v.shape, 0) < 2

    def halves(total, dim):
        two, ahead, behind = (pick(total, dim, d) for d in (2, 1, 3))
        return jnp.where(front(two), two, ahead), jnp.where(front(two), behind, two)

    def both(chunks, dim):
        ring = (x_ring, y_ring)[dim]
        return ring(chunks[0], 1), ring(chunks[1], 3)

    def relayed(total, dim, plus, minus):
        ahead = pick(total, dim, 1)[:2].astype(F32) + plus[:2].astype(F32)
        behind = pick(total, dim, 3)[2:].astype(F32) + minus[2:].astype(F32)
        return both((ahead.astype(F16), behind.astype(F16)), dim)

    def summed(total, dim, plus, minus, ahead, behind):
        got = jnp.where(front(plus), minus, plus).astype(F32)
        got = got + jnp.concatenate([ahead, behind]).astype(F32)
        return pick(total, dim, 0).astype(F32) + got

    total_a = term(near, slice(0, part_a))
    first_a = halves(total_a, 0)
    near = after(first_a, near)
    total_b = term(near, slice(part_a, width))
    first_a = both(first_a, 0)
    first_b = both(halves(total_b, 1), 1)
    one_a = summed(total_a, 0, *first_a, *relayed(total_a, 0, *first_a))[None]
    last_b = relayed(total_b, 1, *first_b)
    chunks_a = cut(one_a, 1)
    last_b = [after(chunks_a, v) for v in last_b]
    two_a = send(chunks_a, 1)
    one_b = summed(total_b, 1, *first_b, *last_b)[:, None]
    two_b = send(cut(one_b, 0), 0)
    two_a = gathered(one_a, 1, two_a)[0].astype(F16)
    two_b = [after([two_a], v) for v in two_b]
    two_b = gathered(one_b, 0, two_b)[0].astype(F16)
    two = [two_a, two_b]
    last = jnp.concatenate(two, axis=1).reshape(NZ, rows * width // 128, 128)
    last = lax.all_to_all(last, "z", 0, 0)
    grad = (last.astype(F32).sum(axis=0) * (1.0 / SCALE)).reshape(rows, width)

    moment_s, second_s, weight_s = adamw(grad[:sr], master_shared, moment_shared, second_shared)
    moment_r, second_r, weight_r = adamw(grad[sr:], master_routed, moment_routed, second_routed)

    weight = jnp.concatenate([weight_s, weight_r], axis=0).reshape(1, rows * width // 128, 128)
    weight = lax.all_to_all(jnp.broadcast_to(weight, (NZ,) + weight.shape[1:]), "z", 0, 0)
    weight_s = weight[:, : sr * width // 128].reshape(NZ * sr, width)
    weight_r = weight[:, sr * width // 128 :].reshape(NZ * rr, width)
    mine, other = weight_s, y_swap(weight_s)
    mine_plus, mine_minus = x_ring(mine, 1), x_ring(mine, 3)
    other_plus, other_minus = x_ring(other, 1), x_ring(other, 3)
    mine_two, other_two = x_ring(mine_plus, 1), x_ring(other_minus, 3)
    around = [after([other, mine_plus], x_ring(weight_r, d)) for d in (1, 2, 3)]
    all_r = jnp.concatenate([weight_r] + around, axis=0)
    all_r = jnp.concatenate([all_r, y_swap(all_r)], axis=0)
    all_s = jnp.concatenate(
        [mine, other, mine_plus, other_plus, mine_two, other_two, mine_minus, other_minus], axis=0
    )

    def settled(full, count, index):
        n = full.shape[0]
        r = lax.iota(jnp.int32, n)
        back = (x - (r // count) % NX) % NX
        zz = (r // (count * NX)) % NZ
        flip = (r // (count * NX * NZ)) ^ yl
        want = lax.optimization_barrier((index(back, flip) * NZ + zz) * count + r % count)
        take = (want[:, None] == lax.broadcasted_iota(jnp.int32, (n, n), 1)).astype(BF)
        return dot(lax.optimization_barrier(take), full).astype(BF)

    shared = settled(all_s, sr, lambda back, flip: back * 2 + flip)
    routed = settled(all_r, rr, lambda back, flip: flip * NX + back)
    return (moment_s, second_s, moment_r, second_r, shared, routed)


def solution(mesh):
    fine = Mesh(mesh.devices.reshape(2, 2, 2, NZ, NX), AXES)
    split = P(AXES, None)
    flat = P(AXES)
    cuts = P(("yh", "core"), None)
    return jax.shard_map(
        local,
        mesh=fine,
        in_specs=(split, split, split, flat, flat) + (split,) * 6,
        out_specs=(split,) * 4 + (cuts,) * 2,
        check_vma=False,
    )
```

```python
import jax
import jax.numpy as jnp
import numpy as np
from jax import lax
from jax.experimental import pallas as pl
from jax.experimental.pallas import tpu as pltpu
from jax.sharding import Mesh, PartitionSpec as P

AXES = ("yh", "core", "yl", "z", "x")
NX, NY, NZ = 4, 4, 8
SCALE = 0.25
BF = jnp.bfloat16
F32 = jnp.float32
F16 = jnp.float16


def adamw(grad, master, moment, second):
    corr_one = 1.0 - 0.9**20
    corr_two = 1.0 - 0.95**20
    new_moment = 0.9 * moment + 0.1 * grad
    new_second = 0.95 * second + 0.05 * grad * grad
    step_dir = new_moment / corr_one / (jnp.sqrt(new_second / corr_two) + 1e-08)
    new_master = master - 0.02 * (step_dir + 0.1 * master)
    return (new_moment, new_second, new_master.astype(BF))


def x_ring(v, d):
    return lax.ppermute(v, "x", [(i, (i + d) % NX) for i in range(NX)])


def y_ring(v, d):
    return lax.ppermute(v, ("yh", "yl"), [(i, (i + d) % NY) for i in range(NY)])


def y_swap(v):
    return lax.ppermute(v, "yl", [(0, 1), (1, 0)])


def core_swap(v):
    return lax.ppermute(v, "core", [(0, 1), (1, 0)])


def after(done, v):
    return lax.optimization_barrier((v, *done))[0]


def row_order(sr, rr):
    rows = sr + rr
    n = NX * 2 * NZ * rows
    xs, ys, zs, i = np.meshgrid(np.arange(NX), np.arange(2), np.arange(NZ), np.arange(rows), indexing="ij")
    dev = (ys * NZ + zs) * NX + xs
    flat = np.arange(n)
    keep = (i < sr).reshape(-1)
    shared = np.zeros((n, 2 * NZ * NX * sr), np.float32)
    shared[flat[keep], (dev * sr + i).reshape(-1)[keep]] = 1
    routed = np.zeros((2, n, 2, 2 * NZ * NX * rr), np.float32)
    for core in range(2):
        routed[core, flat[~keep], core, (dev * rr + i - sr).reshape(-1)[~keep]] = 1
    return shared.astype(BF), routed.reshape(2, n, -1).astype(BF)


def dot_t(a, b):
    return lax.dot_general(a, b, (((1,), (1,)), ((), ())), preferred_element_type=F32)


def dot(a, b):
    return jnp.dot(a, b, preferred_element_type=F32)


def order_kernel(core_ref, count_ref, token_ref, shared_ref, routed_ref, shared_order_ref, routed_order_ref, far, near):
    tok, slots = shared_ref.shape[0], routed_ref.shape[0]
    names = lax.broadcasted_iota(jnp.int32, (tok, slots), 0) == token_ref[...]
    live = lax.broadcasted_iota(jnp.int32, (tok, slots), 1) < count_ref[0]
    place = jnp.where(names & live, 1.0, 0.0).astype(BF)
    slot_rows = dot_t(routed_order_ref[0], routed_ref[...]).astype(BF)
    order = jnp.concatenate([shared_order_ref[...], slot_rows], axis=1)
    total = dot_t(order, jnp.concatenate([shared_ref[...], place], axis=1))

    @pl.when(pl.program_id(0) < 2)
    def _():
        far[...] = total.astype(BF).reshape(far.shape)

    @pl.when(pl.program_id(0) >= 2)
    def _():
        near[...] = total.astype(BF).reshape(near.shape)


def ordered(core, count, token, hid_shared, hid_routed, shared_order, routed_order):
    tok = hid_shared.shape[0]
    slots = hid_routed.shape[0]
    n, cut = shared_order.shape
    pair = routed_order.shape[2]

    def who(j, c):
        return jnp.where(j < 2, 1 - c[0], c[0])

    def out(low):
        return pl.BlockSpec((NX, 1, n // NX, tok), lambda j, c, m: (0, jnp.clip(j - low, 0, 1), 0, 0))

    shape = jax.ShapeDtypeStruct((NX, 2, n // NX, tok), BF)
    return pl.pallas_call(
        order_kernel,
        grid_spec=pltpu.PrefetchScalarGridSpec(
            num_scalar_prefetch=2,
            grid=(4,),
            in_specs=[
                pl.BlockSpec((1, slots), lambda j, c, m: (0, 0)),
                pl.BlockSpec((tok, cut), lambda j, c, m: (0, (j % 2) * 2 + who(j, c))),
                pl.BlockSpec((slots, pair), lambda j, c, m: (0, j % 2)),
                pl.BlockSpec((n, cut), lambda j, c, m: (0, 0)),
                pl.BlockSpec((1, n, pair), lambda j, c, m: (who(j, c), 0, 0)),
            ],
            out_specs=[out(0), out(2)],
        ),
        out_shape=[shape, shape],
        compiler_params=pltpu.CompilerParams(vmem_limit_bytes=56 * 2**20),
        cost_estimate=pl.CostEstimate(flops=16 * n * cut * tok, bytes_accessed=20 * n * tok, transcendentals=0),
    )(core.reshape(1), count, token.reshape(1, slots), hid_shared, hid_routed, shared_order, routed_order)


def local(
    hid_shared,
    hid_routed,
    out_grad,
    slot_token,
    slot_count,
    master_shared,
    moment_shared,
    second_shared,
    master_routed,
    moment_routed,
    second_routed,
):
    tok, width = out_grad.shape
    slots = hid_routed.shape[0]
    sr, rr = master_shared.shape[0], master_routed.shape[0]
    rows = sr + rr
    group = NZ * rows
    core = lax.axis_index("core")
    x = lax.axis_index("x")
    yh, yl = lax.axis_index("yh"), lax.axis_index("yl")
    y = yh * 2 + yl

    shared_order, routed_order = (jnp.asarray(v) for v in row_order(sr, rr))
    part_a = width * 3 // 5
    out_far = core_swap(out_grad)
    far, near = ordered(core, slot_count, slot_token, hid_shared, hid_routed, shared_order, routed_order)
    far = core_swap(far).reshape(-1, tok)
    near = near.reshape(-1, tok)

    def term(near, cols):
        total = dot(near, out_grad[:, cols]) + dot(far, out_far[:, cols])
        return (SCALE * total).astype(F16).reshape(NX, NY, group, -1)

    def pick(v, dim, step):
        index = ((x, y)[dim] + step) % 4
        return lax.dynamic_index_in_dim(v, index, dim, keepdims=False)

    def cut(v, dim):
        return [pick(v, dim, d).astype(F16) for d in (2, 1, 3)]

    def send(chunks, dim):
        return [(x_ring, y_ring)[dim](v, d) for v, d in zip(chunks, (2, 1, 3))]

    def gathered(v, dim, back):
        return sum((b.astype(F32) for b in back), pick(v, dim, 0).astype(F32))

    def front(v):
        return lax.broadcasted_iota(jnp.int32, v.shape, 0) < 2

    def halves(total, dim):
        two, ahead, behind = (pick(total, dim, d) for d in (2, 1, 3))
        return jnp.where(front(two), two, ahead), jnp.where(front(two), behind, two)

    def both(chunks, dim):
        ring = (x_ring, y_ring)[dim]
        return ring(chunks[0], 1), ring(chunks[1], 3)

    def relayed(total, dim, plus, minus):
        ahead = pick(total, dim, 1)[:2].astype(F32) + plus[:2].astype(F32)
        behind = pick(total, dim, 3)[2:].astype(F32) + minus[2:].astype(F32)
        return both((ahead.astype(F16), behind.astype(F16)), dim)

    def summed(total, dim, plus, minus, ahead, behind):
        got = jnp.where(front(plus), minus, plus).astype(F32)
        got = got + jnp.concatenate([ahead, behind]).astype(F32)
        return pick(total, dim, 0).astype(F32) + got

    total_a = term(near, slice(0, part_a))
    first_a = halves(total_a, 0)
    near = after(first_a, near)
    total_b = term(near, slice(part_a, width))
    first_a = both(first_a, 0)
    first_b = both(halves(total_b, 1), 1)
    one_a = summed(total_a, 0, *first_a, *relayed(total_a, 0, *first_a))[None]
    last_b = relayed(total_b, 1, *first_b)
    chunks_a = cut(one_a, 1)
    last_b = [after(chunks_a, v) for v in last_b]
    two_a = send(chunks_a, 1)
    one_b = summed(total_b, 1, *first_b, *last_b)[:, None]
    two_b = lax.all_to_all(one_b[:, 0].astype(F16), "x", 0, 0)
    two_a = gathered(one_a, 1, two_a)[0].astype(F16)
    two_b = after([two_a], two_b).astype(F32).sum(axis=0).astype(F16)
    two = [two_a, two_b]
    last = jnp.concatenate(two, axis=1).reshape(NZ, rows * width // 128, 128)
    last = lax.all_to_all(last, "z", 0, 0)
    grad = (last.astype(F32).sum(axis=0) * (1.0 / SCALE)).reshape(rows, width)

    moment_s, second_s, weight_s = adamw(grad[:sr], master_shared, moment_shared, second_shared)
    moment_r, second_r, weight_r = adamw(grad[sr:], master_routed, moment_routed, second_routed)

    weight = jnp.concatenate([weight_s, weight_r], axis=0).reshape(1, rows * width // 128, 128)
    weight = lax.all_to_all(jnp.broadcast_to(weight, (NZ,) + weight.shape[1:]), "z", 0, 0)
    mine = weight.reshape(group, width)
    part = group // 32 * 16
    mine_plus, mine_minus = x_ring(mine, 1), x_ring(mine, 3)
    other = y_swap(mine)
    two = [x_ring(mine_plus[:part], 1), x_ring(mine_minus[part:], 3)]
    other_plus, other_minus = x_ring(other, 1), x_ring(other, 3)
    mine_two = jnp.concatenate(two, axis=0)
    other_two = y_swap(mine_two)
    full = jnp.concatenate(
        [mine, other, mine_plus, other_plus, mine_two, other_two, mine_minus, other_minus], axis=0
    )

    def settled(count, low):
        n = 2 * NZ * NX * count
        r = lax.iota(jnp.int32, n)
        back = (x - (r // count) % NX) % NX
        zz = (r // (count * NX)) % NZ
        flip = (r // (count * NX * NZ)) ^ yl
        want = ((back * 2 + flip) * NZ + zz) * rows + low + r % count
        want = lax.optimization_barrier(want)
        take = (want[:, None] == lax.broadcasted_iota(jnp.int32, (n, full.shape[0]), 1)).astype(BF)
        return dot(lax.optimization_barrier(take), full).astype(BF)

    shared, routed = settled(sr, 0), settled(rr, sr)
    return (moment_s, second_s, moment_r, second_r, shared, routed)


def solution(mesh):
    fine = Mesh(mesh.devices.reshape(2, 2, 2, NZ, NX), AXES)
    split = P(AXES, None)
    flat = P(AXES)
    cuts = P(("yh", "core"), None)
    return jax.shard_map(
        local,
        mesh=fine,
        in_specs=(split, split, split, flat, flat) + (split,) * 6,
        out_specs=(split,) * 4 + (cuts,) * 2,
        check_vma=False,
    )
```

```python
import jax
import jax.numpy as jnp
import numpy as np
from jax import lax
from jax.experimental import pallas as pl
from jax.experimental.pallas import tpu as pltpu
from jax.sharding import Mesh, PartitionSpec as P

AXES = ("yh", "core", "yl", "z", "x")
NX, NY, NZ = 4, 4, 8
SCALE = 0.25
BF = jnp.bfloat16
F32 = jnp.float32
F16 = jnp.float16


def adamw(grad, master, moment, second):
    corr_one = 1.0 - 0.9**20
    corr_two = 1.0 - 0.95**20
    new_moment = 0.9 * moment + 0.1 * grad
    new_second = 0.95 * second + 0.05 * grad * grad
    step_dir = new_moment / corr_one / (jnp.sqrt(new_second / corr_two) + 1e-08)
    new_master = master - 0.02 * (step_dir + 0.1 * master)
    return (new_moment, new_second, new_master.astype(BF))


def x_ring(v, d):
    return lax.ppermute(v, "x", [(i, (i + d) % NX) for i in range(NX)])


def y_ring(v, d):
    return lax.ppermute(v, ("yh", "yl"), [(i, (i + d) % NY) for i in range(NY)])


def z_ring(v, d):
    return lax.ppermute(v, "z", [(i, (i + d) % NZ) for i in range(NZ)])


def z_swap(v):
    return lax.ppermute(v, "z", [(i, i ^ 1) for i in range(NZ)])


def y_swap(v):
    return lax.ppermute(v, "yl", [(0, 1), (1, 0)])


def core_swap(v):
    return lax.ppermute(v, "core", [(0, 1), (1, 0)])


def after(done, v):
    return lax.optimization_barrier((v, *done))[0]


def row_order(sr, rr):
    rows = sr + rr
    n = NX * 2 * NZ * rows
    xs, ys, zs, i = np.meshgrid(np.arange(NX), np.arange(2), np.arange(NZ), np.arange(rows), indexing="ij")
    dev = (ys * NZ + zs) * NX + xs
    flat = np.arange(n)
    keep = (i < sr).reshape(-1)
    shared = np.zeros((n, 2 * NZ * NX * sr), np.float32)
    shared[flat[keep], (dev * sr + i).reshape(-1)[keep]] = 1
    routed = np.zeros((2, n, 2, 2 * NZ * NX * rr), np.float32)
    for core in range(2):
        routed[core, flat[~keep], core, (dev * rr + i - sr).reshape(-1)[~keep]] = 1
    return shared.astype(BF), routed.reshape(2, n, -1).astype(BF)


def dot_t(a, b):
    return lax.dot_general(a, b, (((1,), (1,)), ((), ())), preferred_element_type=F32)


def dot(a, b):
    return jnp.dot(a, b, preferred_element_type=F32)


def order_kernel(core_ref, count_ref, token_ref, shared_ref, routed_ref, shared_order_ref, routed_order_ref, far, near):
    tok, slots = shared_ref.shape[0], routed_ref.shape[0]
    names = lax.broadcasted_iota(jnp.int32, (tok, slots), 0) == token_ref[...]
    live = lax.broadcasted_iota(jnp.int32, (tok, slots), 1) < count_ref[0]
    place = jnp.where(names & live, 1.0, 0.0).astype(BF)
    slot_rows = dot_t(routed_order_ref[0], routed_ref[...]).astype(BF)
    order = jnp.concatenate([shared_order_ref[...], slot_rows], axis=1)
    total = dot_t(order, jnp.concatenate([shared_ref[...], place], axis=1))

    @pl.when(pl.program_id(0) < 2)
    def _():
        far[...] = total.astype(BF).reshape(far.shape)

    @pl.when(pl.program_id(0) >= 2)
    def _():
        near[...] = total.astype(BF).reshape(near.shape)


def ordered(core, count, token, hid_shared, hid_routed, shared_order, routed_order):
    tok = hid_shared.shape[0]
    slots = hid_routed.shape[0]
    n, cut = shared_order.shape
    pair = routed_order.shape[2]

    def who(j, c):
        return jnp.where(j < 2, 1 - c[0], c[0])

    def out(low):
        return pl.BlockSpec((NX, 1, n // NX, tok), lambda j, c, m: (0, jnp.clip(j - low, 0, 1), 0, 0))

    shape = jax.ShapeDtypeStruct((NX, 2, n // NX, tok), BF)
    return pl.pallas_call(
        order_kernel,
        grid_spec=pltpu.PrefetchScalarGridSpec(
            num_scalar_prefetch=2,
            grid=(4,),
            in_specs=[
                pl.BlockSpec((1, slots), lambda j, c, m: (0, 0)),
                pl.BlockSpec((tok, cut), lambda j, c, m: (0, (j % 2) * 2 + who(j, c))),
                pl.BlockSpec((slots, pair), lambda j, c, m: (0, j % 2)),
                pl.BlockSpec((n, cut), lambda j, c, m: (0, 0)),
                pl.BlockSpec((1, n, pair), lambda j, c, m: (who(j, c), 0, 0)),
            ],
            out_specs=[out(0), out(2)],
        ),
        out_shape=[shape, shape],
        compiler_params=pltpu.CompilerParams(vmem_limit_bytes=56 * 2**20),
        cost_estimate=pl.CostEstimate(flops=16 * n * cut * tok, bytes_accessed=20 * n * tok, transcendentals=0),
    )(core.reshape(1), count, token.reshape(1, slots), hid_shared, hid_routed, shared_order, routed_order)


def local(
    hid_shared,
    hid_routed,
    out_grad,
    slot_token,
    slot_count,
    master_shared,
    moment_shared,
    second_shared,
    master_routed,
    moment_routed,
    second_routed,
):
    tok, width = out_grad.shape
    slots = hid_routed.shape[0]
    sr, rr = master_shared.shape[0], master_routed.shape[0]
    rows = sr + rr
    group = NZ * rows
    core = lax.axis_index("core")
    x = lax.axis_index("x")
    z = lax.axis_index("z")
    yh, yl = lax.axis_index("yh"), lax.axis_index("yl")
    y = yh * 2 + yl

    shared_order, routed_order = (jnp.asarray(v) for v in row_order(sr, rr))
    part_a = width * 3 // 5
    out_far = core_swap(out_grad)
    far, near = ordered(core, slot_count, slot_token, hid_shared, hid_routed, shared_order, routed_order)
    far = core_swap(far).reshape(-1, tok)
    near = near.reshape(-1, tok)

    def term(near, cols):
        total = dot(near, out_grad[:, cols]) + dot(far, out_far[:, cols])
        return (SCALE * total).astype(F16).reshape(NX, NY, group, -1)

    def pick(v, dim, step):
        index = ((x, y)[dim] + step) % 4
        return lax.dynamic_index_in_dim(v, index, dim, keepdims=False)

    def cut(v, dim):
        return [pick(v, dim, d).astype(F16) for d in (2, 1, 3)]

    def send(chunks, dim):
        return [(x_ring, y_ring)[dim](v, d) for v, d in zip(chunks, (2, 1, 3))]

    def gathered(v, dim, back):
        return sum((b.astype(F32) for b in back), pick(v, dim, 0).astype(F32))

    def front(v):
        return lax.broadcasted_iota(jnp.int32, v.shape, 0) < 2

    def halves(total, dim):
        two, ahead, behind = (pick(total, dim, d) for d in (2, 1, 3))
        return jnp.where(front(two), two, ahead), jnp.where(front(two), behind, two)

    def both(chunks, dim):
        ring = (x_ring, y_ring)[dim]
        return ring(chunks[0], 1), ring(chunks[1], 3)

    def relayed(total, dim, plus, minus):
        ahead = pick(total, dim, 1)[:2].astype(F32) + plus[:2].astype(F32)
        behind = pick(total, dim, 3)[2:].astype(F32) + minus[2:].astype(F32)
        return both((ahead.astype(F16), behind.astype(F16)), dim)

    def summed(total, dim, plus, minus, ahead, behind):
        got = jnp.where(front(plus), minus, plus).astype(F32)
        got = got + jnp.concatenate([ahead, behind]).astype(F32)
        return pick(total, dim, 0).astype(F32) + got

    total_a = term(near, slice(0, part_a))
    first_a = halves(total_a, 0)
    near = after(first_a, near)
    total_b = term(near, slice(part_a, width))
    first_a = both(first_a, 0)
    first_b = both(halves(total_b, 1), 1)
    one_a = summed(total_a, 0, *first_a, *relayed(total_a, 0, *first_a))[None]
    last_b = relayed(total_b, 1, *first_b)
    chunks_a = cut(one_a, 1)
    last_b = [after(chunks_a, v) for v in last_b]
    two_a = send(chunks_a, 1)
    one_b = summed(total_b, 1, *first_b, *last_b)[:, None]
    two_b = send(cut(one_b, 0), 0)
    two_a = gathered(one_a, 1, two_a)[0].astype(F16)
    two_b = [after([two_a], v) for v in two_b]
    two_b = gathered(one_b, 0, two_b)[0].astype(F16)
    two = [two_a, two_b]
    last = jnp.concatenate(two, axis=1).reshape(NZ, rows * width // 128, 128)
    last = lax.all_to_all(last, "z", 0, 0)
    grad = (last.astype(F32).sum(axis=0) * (1.0 / SCALE)).reshape(rows, width)

    moment_s, second_s, weight_s = adamw(grad[:sr], master_shared, moment_shared, second_shared)
    moment_r, second_r, weight_r = adamw(grad[sr:], master_routed, moment_routed, second_routed)

    weight = jnp.concatenate([weight_s, weight_r], axis=0).reshape(rows * width // 128, 128)
    mine = jnp.concatenate([weight] + [z_ring(weight, d) for d in (2, 4, 6)], axis=0)
    mine = jnp.concatenate([mine, z_swap(mine)], axis=0).reshape(group, width)
    part = group // 32 * 16
    mine_plus, mine_minus = x_ring(mine, 1), x_ring(mine, 3)
    other = y_swap(mine)
    two = [x_ring(mine_plus[:part], 1), x_ring(mine_minus[part:], 3)]
    other_plus, other_minus = x_ring(other, 1), x_ring(other, 3)
    mine_two = jnp.concatenate(two, axis=0)
    other_two = y_swap(mine_two)
    early = jnp.concatenate([mine, mine_plus, mine_minus, other, mine_two], axis=0)
    late = [other_plus, other_minus, other_two]
    slot = jnp.array([0, 1, 4, 2, 3, 5, 7, 6], jnp.int32)

    def wanted(count, low):
        n = 2 * NZ * NX * count
        r = lax.iota(jnp.int32, n)
        back = (x - (r // count) % NX) % NX
        zz = (r // (count * NX)) % NZ
        flip = (r // (count * NX * NZ)) ^ yl
        odd = (zz ^ z) & 1
        steps = ((z ^ odd) - zz) % NZ // 2
        block = slot[flip * NX + back]
        want = (block * NZ + odd * (NZ // 2) + steps) * rows + low + r % count
        return lax.optimization_barrier(want)

    def take(want, start, full):
        q = lax.broadcasted_iota(jnp.int32, (want.shape[0], full.shape[0]), 1) + start
        return dot(lax.optimization_barrier((want[:, None] == q).astype(BF)), full)

    wants = [wanted(sr, 0), wanted(rr, sr)]
    firsts = [take(want, 0, early) for want in wants]
    late = jnp.concatenate([after(firsts, v) for v in late], axis=0)
    shared, routed = ((f + take(want, early.shape[0], late)).astype(BF) for f, want in zip(firsts, wants))
    return (moment_s, second_s, moment_r, second_r, shared, routed)


def solution(mesh):
    fine = Mesh(mesh.devices.reshape(2, 2, 2, NZ, NX), AXES)
    split = P(AXES, None)
    flat = P(AXES)
    cuts = P(("yh", "core"), None)
    return jax.shard_map(
        local,
        mesh=fine,
        in_specs=(split, split, split, flat, flat) + (split,) * 6,
        out_specs=(split,) * 4 + (cuts,) * 2,
        check_vma=False,
    )
```

```python
import jax
import jax.numpy as jnp
import numpy as np
from jax import lax
from jax.experimental import pallas as pl
from jax.experimental.pallas import tpu as pltpu
from jax.sharding import Mesh, PartitionSpec as P

AXES = ("yh", "core", "yl", "z", "x")
NX, NY, NZ = 4, 4, 8
SCALE = 0.25
BF = jnp.bfloat16
F32 = jnp.float32
F16 = jnp.float16


def adamw(grad, master, moment, second):
    corr_one = 1.0 - 0.9**20
    corr_two = 1.0 - 0.95**20
    new_moment = 0.9 * moment + 0.1 * grad
    new_second = 0.95 * second + 0.05 * grad * grad
    step_dir = new_moment / corr_one / (jnp.sqrt(new_second / corr_two) + 1e-08)
    new_master = master - 0.02 * (step_dir + 0.1 * master)
    return (new_moment, new_second, new_master.astype(BF))


def x_ring(v, d):
    return lax.ppermute(v, "x", [(i, (i + d) % NX) for i in range(NX)])


def y_ring(v, d):
    return lax.ppermute(v, ("yh", "yl"), [(i, (i + d) % NY) for i in range(NY)])


def y_swap(v):
    return lax.ppermute(v, "yl", [(0, 1), (1, 0)])


def core_swap(v):
    return lax.ppermute(v, "core", [(0, 1), (1, 0)])


def after(done, v):
    return lax.optimization_barrier((v, *done))[0]


def row_order(sr, rr):
    rows = sr + rr
    n = NX * 2 * NZ * rows
    xs, ys, zs, i = np.meshgrid(np.arange(NX), np.arange(2), np.arange(NZ), np.arange(rows), indexing="ij")
    dev = (ys * NZ + zs) * NX + xs
    flat = np.arange(n)
    keep = (i < sr).reshape(-1)
    shared = np.zeros((n, 2 * NZ * NX * sr), np.float32)
    shared[flat[keep], (dev * sr + i).reshape(-1)[keep]] = 1
    routed = np.zeros((2, n, 2, 2 * NZ * NX * rr), np.float32)
    for core in range(2):
        routed[core, flat[~keep], core, (dev * rr + i - sr).reshape(-1)[~keep]] = 1
    return shared.astype(BF), routed.reshape(2, n, -1).astype(BF)


def dot_t(a, b):
    return lax.dot_general(a, b, (((1,), (1,)), ((), ())), preferred_element_type=F32)


def dot(a, b):
    return jnp.dot(a, b, preferred_element_type=F32)


def order_kernel(core_ref, count_ref, token_ref, shared_ref, routed_ref, shared_order_ref, routed_order_ref, far, near):
    tok, slots = shared_ref.shape[0], routed_ref.shape[0]
    names = lax.broadcasted_iota(jnp.int32, (tok, slots), 0) == token_ref[...]
    live = lax.broadcasted_iota(jnp.int32, (tok, slots), 1) < count_ref[0]
    place = jnp.where(names & live, 1.0, 0.0).astype(BF)
    slot_rows = dot_t(routed_order_ref[0], routed_ref[...]).astype(BF)
    order = jnp.concatenate([shared_order_ref[...], slot_rows], axis=1)
    total = dot_t(order, jnp.concatenate([shared_ref[...], place], axis=1))

    @pl.when(pl.program_id(0) < 2)
    def _():
        far[...] = total.astype(BF).reshape(far.shape)

    @pl.when(pl.program_id(0) >= 2)
    def _():
        near[...] = total.astype(BF).reshape(near.shape)


def ordered(core, count, token, hid_shared, hid_routed, shared_order, routed_order):
    tok = hid_shared.shape[0]
    slots = hid_routed.shape[0]
    n, cut = shared_order.shape
    pair = routed_order.shape[2]

    def who(j, c):
        return jnp.where(j < 2, 1 - c[0], c[0])

    def out(low):
        return pl.BlockSpec((NX, 1, n // NX, tok), lambda j, c, m: (0, jnp.clip(j - low, 0, 1), 0, 0))

    shape = jax.ShapeDtypeStruct((NX, 2, n // NX, tok), BF)
    return pl.pallas_call(
        order_kernel,
        grid_spec=pltpu.PrefetchScalarGridSpec(
            num_scalar_prefetch=2,
            grid=(4,),
            in_specs=[
                pl.BlockSpec((1, slots), lambda j, c, m: (0, 0)),
                pl.BlockSpec((tok, cut), lambda j, c, m: (0, (j % 2) * 2 + who(j, c))),
                pl.BlockSpec((slots, pair), lambda j, c, m: (0, j % 2)),
                pl.BlockSpec((n, cut), lambda j, c, m: (0, 0)),
                pl.BlockSpec((1, n, pair), lambda j, c, m: (who(j, c), 0, 0)),
            ],
            out_specs=[out(0), out(2)],
        ),
        out_shape=[shape, shape],
        compiler_params=pltpu.CompilerParams(vmem_limit_bytes=56 * 2**20),
        cost_estimate=pl.CostEstimate(flops=16 * n * cut * tok, bytes_accessed=20 * n * tok, transcendentals=0),
    )(core.reshape(1), count, token.reshape(1, slots), hid_shared, hid_routed, shared_order, routed_order)


def local(
    hid_shared,
    hid_routed,
    out_grad,
    slot_token,
    slot_count,
    master_shared,
    moment_shared,
    second_shared,
    master_routed,
    moment_routed,
    second_routed,
):
    tok, width = out_grad.shape
    slots = hid_routed.shape[0]
    sr, rr = master_shared.shape[0], master_routed.shape[0]
    rows = sr + rr
    group = NZ * rows
    core = lax.axis_index("core")
    x = lax.axis_index("x")
    yh, yl = lax.axis_index("yh"), lax.axis_index("yl")
    y = yh * 2 + yl

    shared_order, routed_order = (jnp.asarray(v) for v in row_order(sr, rr))
    part_a = width * 11 // 20
    out_far = core_swap(out_grad)
    far, near = ordered(core, slot_count, slot_token, hid_shared, hid_routed, shared_order, routed_order)
    far = core_swap(far).reshape(-1, tok)
    near = near.reshape(-1, tok)

    def term(near, cols):
        total = dot(near, out_grad[:, cols]) + dot(far, out_far[:, cols])
        return (SCALE * total).astype(F16).reshape(NX, NY, group, -1)

    def pick(v, dim, step):
        index = ((x, y)[dim] + step) % 4
        return lax.dynamic_index_in_dim(v, index, dim, keepdims=False)

    def cut(v, dim):
        return [pick(v, dim, d).astype(F16) for d in (2, 1, 3)]

    def send(chunks, dim):
        return [(x_ring, y_ring)[dim](v, d) for v, d in zip(chunks, (2, 1, 3))]

    def gathered(v, dim, back):
        return sum((b.astype(F32) for b in back), pick(v, dim, 0).astype(F32))

    def front(v):
        return lax.broadcasted_iota(jnp.int32, v.shape, 0) < 2

    def halves(total, dim):
        two, ahead, behind = (pick(total, dim, d) for d in (2, 1, 3))
        return jnp.where(front(two), two, ahead), jnp.where(front(two), behind, two)

    def both(chunks, dim):
        ring = (x_ring, y_ring)[dim]
        return ring(chunks[0], 1), ring(chunks[1], 3)

    def relayed(total, dim, plus, minus):
        ahead = pick(total, dim, 1)[:2].astype(F32) + plus[:2].astype(F32)
        behind = pick(total, dim, 3)[2:].astype(F32) + minus[2:].astype(F32)
        return ahead.astype(F16), behind.astype(F16)

    def summed(total, dim, plus, minus, ahead, behind):
        got = jnp.where(front(plus), minus, plus).astype(F32)
        got = got + jnp.concatenate([ahead, behind]).astype(F32)
        return pick(total, dim, 0).astype(F32) + got

    total_a = term(near, slice(0, part_a))
    first_a = halves(total_a, 0)
    near = after(first_a, near)
    total_b = term(near, slice(part_a, width))
    first_a = both(first_a, 0)
    first_b = both(halves(total_b, 1), 1)
    last_a = relayed(total_a, 0, *first_a)
    first_b = [after(last_a, v) for v in first_b]
    one_a = summed(total_a, 0, *first_a, *both(last_a, 0))[None]
    last_b = both(relayed(total_b, 1, *first_b), 1)
    chunks_a = cut(one_a, 1)
    last_b = [after(chunks_a, v) for v in last_b]
    two_a = send(chunks_a, 1)
    one_b = summed(total_b, 1, *first_b, *last_b)[:, None]
    two_b = send(cut(one_b, 0), 0)
    two_a = gathered(one_a, 1, two_a)[0].astype(F16)
    two_b = [after([two_a], v) for v in two_b]
    two_b = gathered(one_b, 0, two_b)[0].astype(F16)
    two = [two_a, two_b]
    last = jnp.concatenate(two, axis=1).reshape(NZ, rows * width // 128, 128)
    last = lax.all_to_all(last, "z", 0, 0)
    grad = (last.astype(F32).sum(axis=0) * (1.0 / SCALE)).reshape(rows, width)

    moment_s, second_s, weight_s = adamw(grad[:sr], master_shared, moment_shared, second_shared)
    moment_r, second_r, weight_r = adamw(grad[sr:], master_routed, moment_routed, second_routed)

    weight = jnp.concatenate([weight_s, weight_r], axis=0).reshape(1, rows * width // 128, 128)
    weight = lax.all_to_all(jnp.broadcast_to(weight, (NZ,) + weight.shape[1:]), "z", 0, 0)
    mine = weight.reshape(group, width)
    part = group // 32 * 16
    mine_plus, mine_minus = x_ring(mine, 1), x_ring(mine, 3)
    other = y_swap(mine)
    two = [x_ring(mine_plus[:part], 1), x_ring(mine_minus[part:], 3)]
    other_plus, other_minus = x_ring(other, 1), x_ring(other, 3)
    mine_two = jnp.concatenate(two, axis=0)
    other_two = y_swap(mine_two)
    early = jnp.concatenate([mine, mine_plus, mine_minus, other, mine_two], axis=0)
    late = [other_plus, other_minus, other_two]
    slot = jnp.array([0, 1, 4, 2, 3, 5, 7, 6], jnp.int32)

    def wanted(count, low):
        n = 2 * NZ * NX * count
        r = lax.iota(jnp.int32, n)
        back = (x - (r // count) % NX) % NX
        zz = (r // (count * NX)) % NZ
        flip = (r // (count * NX * NZ)) ^ yl
        block = slot[flip * NX + back]
        want = (block * NZ + zz) * rows + low + r % count
        return lax.optimization_barrier(want)

    def take(want, start, full):
        q = lax.broadcasted_iota(jnp.int32, (want.shape[0], full.shape[0]), 1) + start
        return dot(lax.optimization_barrier((want[:, None] == q).astype(BF)), full)

    wants = [wanted(sr, 0), wanted(rr, sr)]
    firsts = [take(want, 0, early) for want in wants]
    late = jnp.concatenate([after(firsts, v) for v in late], axis=0)
    shared, routed = ((f + take(want, early.shape[0], late)).astype(BF) for f, want in zip(firsts, wants))
    return (moment_s, second_s, moment_r, second_r, shared, routed)


def solution(mesh):
    fine = Mesh(mesh.devices.reshape(2, 2, 2, NZ, NX), AXES)
    split = P(AXES, None)
    flat = P(AXES)
    cuts = P(("yh", "core"), None)
    return jax.shard_map(
        local,
        mesh=fine,
        in_specs=(split, split, split, flat, flat) + (split,) * 6,
        out_specs=(split,) * 4 + (cuts,) * 2,
        check_vma=False,
    )
```

```python
import jax
import jax.numpy as jnp
import numpy as np
from jax import lax
from jax.experimental import pallas as pl
from jax.experimental.pallas import tpu as pltpu
from jax.sharding import Mesh, PartitionSpec as P

AXES = ("yh", "core", "yl", "z", "x")
NX, NY, NZ = 4, 4, 8
SCALE = 0.25
BF = jnp.bfloat16
F32 = jnp.float32
F16 = jnp.float16


def adamw(grad, master, moment, second):
    corr_one = 1.0 - 0.9**20
    corr_two = 1.0 - 0.95**20
    new_moment = 0.9 * moment + 0.1 * grad
    new_second = 0.95 * second + 0.05 * grad * grad
    step_dir = new_moment / corr_one / (jnp.sqrt(new_second / corr_two) + 1e-08)
    new_master = master - 0.02 * (step_dir + 0.1 * master)
    return (new_moment, new_second, new_master.astype(BF))


def x_ring(v, d):
    return lax.ppermute(v, "x", [(i, (i + d) % NX) for i in range(NX)])


def y_ring(v, d):
    return lax.ppermute(v, ("yh", "yl"), [(i, (i + d) % NY) for i in range(NY)])


def y_swap(v):
    return lax.ppermute(v, "yl", [(0, 1), (1, 0)])


def core_swap(v):
    return lax.ppermute(v, "core", [(0, 1), (1, 0)])


def after(done, v):
    return lax.optimization_barrier((v, *done))[0]


def row_order(sr, rr):
    rows = sr + rr
    n = NX * 2 * NZ * rows
    xs, ys, zs, i = np.meshgrid(np.arange(NX), np.arange(2), np.arange(NZ), np.arange(rows), indexing="ij")
    dev = (ys * NZ + zs) * NX + xs
    flat = np.arange(n)
    keep = (i < sr).reshape(-1)
    shared = np.zeros((n, 2 * NZ * NX * sr), np.float32)
    shared[flat[keep], (dev * sr + i).reshape(-1)[keep]] = 1
    routed = np.zeros((2, n, 2, 2 * NZ * NX * rr), np.float32)
    for core in range(2):
        routed[core, flat[~keep], core, (dev * rr + i - sr).reshape(-1)[~keep]] = 1
    return shared.astype(BF), routed.reshape(2, n, -1).astype(BF)


def dot_t(a, b):
    return lax.dot_general(a, b, (((1,), (1,)), ((), ())), preferred_element_type=F32)


def dot(a, b):
    return jnp.dot(a, b, preferred_element_type=F32)


def order_kernel(core_ref, count_ref, token_ref, shared_ref, routed_ref, shared_order_ref, routed_order_ref, far, near):
    tok, slots = shared_ref.shape[0], routed_ref.shape[0]
    names = lax.broadcasted_iota(jnp.int32, (tok, slots), 0) == token_ref[...]
    live = lax.broadcasted_iota(jnp.int32, (tok, slots), 1) < count_ref[0]
    place = jnp.where(names & live, 1.0, 0.0).astype(BF)
    slot_rows = dot_t(routed_order_ref[0], routed_ref[...]).astype(BF)
    order = jnp.concatenate([shared_order_ref[...], slot_rows], axis=1)
    total = dot_t(order, jnp.concatenate([shared_ref[...], place], axis=1))

    @pl.when(pl.program_id(0) < 2)
    def _():
        far[...] = total.astype(BF).reshape(far.shape)

    @pl.when(pl.program_id(0) >= 2)
    def _():
        near[...] = total.astype(BF).reshape(near.shape)


def ordered(core, count, token, hid_shared, hid_routed, shared_order, routed_order):
    tok = hid_shared.shape[0]
    slots = hid_routed.shape[0]
    n, cut = shared_order.shape
    pair = routed_order.shape[2]

    def who(j, c):
        return jnp.where(j < 2, 1 - c[0], c[0])

    def out(low):
        return pl.BlockSpec((NX, 1, n // NX, tok), lambda j, c, m: (0, jnp.clip(j - low, 0, 1), 0, 0))

    shape = jax.ShapeDtypeStruct((NX, 2, n // NX, tok), BF)
    return pl.pallas_call(
        order_kernel,
        grid_spec=pltpu.PrefetchScalarGridSpec(
            num_scalar_prefetch=2,
            grid=(4,),
            in_specs=[
                pl.BlockSpec((1, slots), lambda j, c, m: (0, 0)),
                pl.BlockSpec((tok, cut), lambda j, c, m: (0, (j % 2) * 2 + who(j, c))),
                pl.BlockSpec((slots, pair), lambda j, c, m: (0, j % 2)),
                pl.BlockSpec((n, cut), lambda j, c, m: (0, 0)),
                pl.BlockSpec((1, n, pair), lambda j, c, m: (who(j, c), 0, 0)),
            ],
            out_specs=[out(0), out(2)],
        ),
        out_shape=[shape, shape],
        compiler_params=pltpu.CompilerParams(vmem_limit_bytes=56 * 2**20),
        cost_estimate=pl.CostEstimate(flops=16 * n * cut * tok, bytes_accessed=20 * n * tok, transcendentals=0),
    )(core.reshape(1), count, token.reshape(1, slots), hid_shared, hid_routed, shared_order, routed_order)


def local(
    hid_shared,
    hid_routed,
    out_grad,
    slot_token,
    slot_count,
    master_shared,
    moment_shared,
    second_shared,
    master_routed,
    moment_routed,
    second_routed,
):
    tok, width = out_grad.shape
    slots = hid_routed.shape[0]
    sr, rr = master_shared.shape[0], master_routed.shape[0]
    rows = sr + rr
    group = NZ * rows
    core = lax.axis_index("core")
    x = lax.axis_index("x")
    yh, yl = lax.axis_index("yh"), lax.axis_index("yl")
    y = yh * 2 + yl

    shared_order, routed_order = (jnp.asarray(v) for v in row_order(sr, rr))
    part_a = width * 11 // 20
    out_far = core_swap(out_grad)
    far, near = ordered(core, slot_count, slot_token, hid_shared, hid_routed, shared_order, routed_order)
    far = core_swap(far).reshape(-1, tok)
    near = near.reshape(-1, tok)

    def term(near, cols):
        total = dot(near, out_grad[:, cols]) + dot(far, out_far[:, cols])
        return (SCALE * total).astype(F16).reshape(NX, NY, group, -1)

    def pick(v, dim, step):
        index = ((x, y)[dim] + step) % 4
        return lax.dynamic_index_in_dim(v, index, dim, keepdims=False)

    def cut(v, dim):
        return [pick(v, dim, d).astype(F16) for d in (2, 1, 3)]

    def send(chunks, dim):
        return [(x_ring, y_ring)[dim](v, d) for v, d in zip(chunks, (2, 1, 3))]

    def gathered(v, dim, back):
        return sum((b.astype(F32) for b in back), pick(v, dim, 0).astype(F32))

    def front(v):
        return lax.broadcasted_iota(jnp.int32, v.shape, 0) < 2

    def halves(total, dim):
        two, ahead, behind = (pick(total, dim, d) for d in (2, 1, 3))
        return jnp.where(front(two), two, ahead), jnp.where(front(two), behind, two)

    def both(chunks, dim):
        ring = (x_ring, y_ring)[dim]
        return ring(chunks[0], 1), ring(chunks[1], 3)

    def relayed(total, dim, plus, minus):
        ahead = pick(total, dim, 1)[:2].astype(F32) + plus[:2].astype(F32)
        behind = pick(total, dim, 3)[2:].astype(F32) + minus[2:].astype(F32)
        return ahead.astype(F16), behind.astype(F16)

    def summed(total, dim, plus, minus, ahead, behind):
        got = jnp.where(front(plus), minus, plus).astype(F32)
        got = got + jnp.concatenate([ahead, behind]).astype(F32)
        return pick(total, dim, 0).astype(F32) + got

    total_a = term(near, slice(0, part_a))
    first_a = halves(total_a, 0)
    near = after(first_a, near)
    total_b = term(near, slice(part_a, width))
    first_a = both(first_a, 0)
    first_b = both(halves(total_b, 1), 1)
    last_a = relayed(total_a, 0, *first_a)
    first_b = [after(last_a, v) for v in first_b]
    one_a = summed(total_a, 0, *first_a, *both(last_a, 0))[None]
    last_b = both(relayed(total_b, 1, *first_b), 1)
    chunks_a = cut(one_a, 1)
    last_b = [after(chunks_a, v) for v in last_b]
    two_a = send(chunks_a, 1)
    one_b = summed(total_b, 1, *first_b, *last_b)[:, None]
    two_b = send(cut(one_b, 0), 0)
    two_a = gathered(one_a, 1, two_a)[0].astype(F16)
    two_b = [after([two_a], v) for v in two_b]
    two_b = gathered(one_b, 0, two_b)[0].astype(F16)
    two = [two_a, two_b]
    last = jnp.concatenate(two, axis=1).reshape(NZ, rows * width // 128, 128)
    last = lax.all_to_all(last, "z", 0, 0)
    grad = (last.astype(F32).sum(axis=0) * (1.0 / SCALE)).reshape(rows, width)

    moment_s, second_s, weight_s = adamw(grad[:sr], master_shared, moment_shared, second_shared)
    moment_r, second_r, weight_r = adamw(grad[sr:], master_routed, moment_routed, second_routed)

    weight = jnp.concatenate([weight_s, weight_r], axis=0).reshape(1, rows * width // 128, 128)
    weight = lax.all_to_all(jnp.broadcast_to(weight, (NZ,) + weight.shape[1:]), "z", 0, 0)
    mine = weight.reshape(group, width)
    part = group // 32 * 16
    mine_plus, mine_minus = x_ring(mine, 1), x_ring(mine, 3)
    other = y_swap(mine)
    two = [x_ring(mine_plus[:part], 1), x_ring(mine_minus[part:], 3)]
    other_plus, other_minus = x_ring(other, 1), x_ring(other, 3)
    mine_two = jnp.concatenate(two, axis=0)
    other_two = y_swap(mine_two)
    early = jnp.concatenate([mine, mine_plus, mine_minus, other, mine_two], axis=0)
    late = [other_plus, other_minus, other_two]
    slot = jnp.array([0, 1, 4, 2, 3, 5, 7, 6], jnp.int32)

    def wanted(count, low):
        n = 2 * NZ * NX * count
        r = after([weight_s, weight_r], lax.iota(jnp.int32, n))
        back = (x - (r // count) % NX) % NX
        zz = (r // (count * NX)) % NZ
        flip = (r // (count * NX * NZ)) ^ yl
        block = slot[flip * NX + back]
        want = (block * NZ + zz) * rows + low + r % count
        return lax.optimization_barrier(want)

    def take(want, start, full):
        want = lax.optimization_barrier(want - start)
        q = lax.broadcasted_iota(jnp.int32, (want.shape[0], full.shape[0]), 1)
        return dot(lax.optimization_barrier((want[:, None] == q).astype(BF)), full).astype(BF)

    wants = [wanted(sr, 0), wanted(rr, sr)]
    firsts = [take(want, 0, early) for want in wants]
    late = jnp.concatenate([after(firsts, v) for v in late], axis=0)
    shared, routed = (f + take(want, early.shape[0], late) for f, want in zip(firsts, wants))
    return (moment_s, second_s, moment_r, second_r, shared, routed)


def solution(mesh):
    fine = Mesh(mesh.devices.reshape(2, 2, 2, NZ, NX), AXES)
    split = P(AXES, None)
    flat = P(AXES)
    cuts = P(("yh", "core"), None)
    return jax.shard_map(
        local,
        mesh=fine,
        in_specs=(split, split, split, flat, flat) + (split,) * 6,
        out_specs=(split,) * 4 + (cuts,) * 2,
        check_vma=False,
    )
```

```python
import jax
import jax.numpy as jnp
import numpy as np
from jax import lax
from jax.experimental import pallas as pl
from jax.experimental.pallas import tpu as pltpu
from jax.sharding import Mesh, PartitionSpec as P

AXES = ("yh", "core", "yl", "z", "x")
NX, NY, NZ = 4, 4, 8
SCALE = 0.25
BF = jnp.bfloat16
F32 = jnp.float32
F16 = jnp.float16


def adamw(grad, master, moment, second):
    corr_one = 1.0 - 0.9**20
    corr_two = 1.0 - 0.95**20
    new_moment = 0.9 * moment + 0.1 * grad
    new_second = 0.95 * second + 0.05 * grad * grad
    step_dir = new_moment / corr_one / (jnp.sqrt(new_second / corr_two) + 1e-08)
    new_master = master - 0.02 * (step_dir + 0.1 * master)
    return (new_moment, new_second, new_master.astype(BF))


def x_ring(v, d):
    return lax.ppermute(v, "x", [(i, (i + d) % NX) for i in range(NX)])


def y_ring(v, d):
    return lax.ppermute(v, ("yh", "yl"), [(i, (i + d) % NY) for i in range(NY)])


def y_swap(v):
    return lax.ppermute(v, "yl", [(0, 1), (1, 0)])


def core_swap(v):
    return lax.ppermute(v, "core", [(0, 1), (1, 0)])


def after(done, v):
    return lax.optimization_barrier((v, *done))[0]


def row_order(sr, rr):
    rows = sr + rr
    n = NX * 2 * NZ * rows
    xs, ys, zs, i = np.meshgrid(np.arange(NX), np.arange(2), np.arange(NZ), np.arange(rows), indexing="ij")
    dev = (ys * NZ + zs) * NX + xs
    flat = np.arange(n)
    keep = (i < sr).reshape(-1)
    shared = np.zeros((n, 2 * NZ * NX * sr), np.float32)
    shared[flat[keep], (dev * sr + i).reshape(-1)[keep]] = 1
    routed = np.zeros((2, n, 2, 2 * NZ * NX * rr), np.float32)
    for core in range(2):
        routed[core, flat[~keep], core, (dev * rr + i - sr).reshape(-1)[~keep]] = 1
    return shared.astype(BF), routed.reshape(2, n, -1).astype(BF)


def dot_t(a, b):
    return lax.dot_general(a, b, (((1,), (1,)), ((), ())), preferred_element_type=F32)


def dot(a, b):
    return jnp.dot(a, b, preferred_element_type=F32)


def order_kernel(core_ref, count_ref, token_ref, shared_ref, routed_ref, shared_order_ref, routed_order_ref, far, near):
    tok, slots = shared_ref.shape[0], routed_ref.shape[0]
    names = lax.broadcasted_iota(jnp.int32, (tok, slots), 0) == token_ref[...]
    live = lax.broadcasted_iota(jnp.int32, (tok, slots), 1) < count_ref[0]
    place = jnp.where(names & live, 1.0, 0.0).astype(BF)
    slot_rows = dot_t(routed_order_ref[0], routed_ref[...]).astype(BF)
    order = jnp.concatenate([shared_order_ref[...], slot_rows], axis=1)
    total = dot_t(order, jnp.concatenate([shared_ref[...], place], axis=1))

    @pl.when(pl.program_id(0) < 2)
    def _():
        far[...] = total.astype(BF).reshape(far.shape)

    @pl.when(pl.program_id(0) >= 2)
    def _():
        near[...] = total.astype(BF).reshape(near.shape)


def ordered(core, count, token, hid_shared, hid_routed, shared_order, routed_order):
    tok = hid_shared.shape[0]
    slots = hid_routed.shape[0]
    n, cut = shared_order.shape
    pair = routed_order.shape[2]

    def who(j, c):
        return jnp.where(j < 2, 1 - c[0], c[0])

    def out(low):
        return pl.BlockSpec((NX, 1, n // NX, tok), lambda j, c, m: (0, jnp.clip(j - low, 0, 1), 0, 0))

    shape = jax.ShapeDtypeStruct((NX, 2, n // NX, tok), BF)
    return pl.pallas_call(
        order_kernel,
        grid_spec=pltpu.PrefetchScalarGridSpec(
            num_scalar_prefetch=2,
            grid=(4,),
            in_specs=[
                pl.BlockSpec((1, slots), lambda j, c, m: (0, 0)),
                pl.BlockSpec((tok, cut), lambda j, c, m: (0, (j % 2) * 2 + who(j, c))),
                pl.BlockSpec((slots, pair), lambda j, c, m: (0, j % 2)),
                pl.BlockSpec((n, cut), lambda j, c, m: (0, 0)),
                pl.BlockSpec((1, n, pair), lambda j, c, m: (who(j, c), 0, 0)),
            ],
            out_specs=[out(0), out(2)],
        ),
        out_shape=[shape, shape],
        compiler_params=pltpu.CompilerParams(vmem_limit_bytes=56 * 2**20),
        cost_estimate=pl.CostEstimate(flops=16 * n * cut * tok, bytes_accessed=20 * n * tok, transcendentals=0),
    )(core.reshape(1), count, token.reshape(1, slots), hid_shared, hid_routed, shared_order, routed_order)


def local(
    hid_shared,
    hid_routed,
    out_grad,
    slot_token,
    slot_count,
    master_shared,
    moment_shared,
    second_shared,
    master_routed,
    moment_routed,
    second_routed,
):
    tok, width = out_grad.shape
    slots = hid_routed.shape[0]
    sr, rr = master_shared.shape[0], master_routed.shape[0]
    rows = sr + rr
    group = NZ * rows
    core = lax.axis_index("core")
    x = lax.axis_index("x")
    yh, yl = lax.axis_index("yh"), lax.axis_index("yl")
    y = yh * 2 + yl

    shared_order, routed_order = (jnp.asarray(v) for v in row_order(sr, rr))
    part_a = width * 11 // 20
    out_far = core_swap(out_grad)
    far, near = ordered(core, slot_count, slot_token, hid_shared, hid_routed, shared_order, routed_order)
    far = core_swap(far).reshape(-1, tok)
    near = near.reshape(-1, tok)

    def term(near, cols):
        total = dot(near, out_grad[:, cols]) + dot(far, out_far[:, cols])
        return (SCALE * total).astype(F16).reshape(NX, NY, group, -1)

    def pick(v, dim, step):
        index = ((x, y)[dim] + step) % 4
        return lax.dynamic_index_in_dim(v, index, dim, keepdims=False)

    def cut(v, dim):
        return [pick(v, dim, d).astype(F16) for d in (2, 1, 3)]

    def send(chunks, dim):
        return [(x_ring, y_ring)[dim](v, d) for v, d in zip(chunks, (2, 1, 3))]

    def gathered(v, dim, back):
        return sum((b.astype(F32) for b in back), pick(v, dim, 0).astype(F32))

    def front(v):
        return lax.broadcasted_iota(jnp.int32, v.shape, 0) < 2

    def halves(total, dim):
        two, ahead, behind = (pick(total, dim, d) for d in (2, 1, 3))
        return jnp.where(front(two), two, ahead), jnp.where(front(two), behind, two)

    def both(chunks, dim):
        ring = (x_ring, y_ring)[dim]
        return ring(chunks[0], 1), ring(chunks[1], 3)

    def relayed(total, dim, plus, minus):
        ahead = pick(total, dim, 1)[:2].astype(F32) + plus[:2].astype(F32)
        behind = pick(total, dim, 3)[2:].astype(F32) + minus[2:].astype(F32)
        return ahead.astype(F16), behind.astype(F16)

    def summed(total, dim, plus, minus, ahead, behind):
        got = jnp.where(front(plus), minus, plus).astype(F32)
        got = got + jnp.concatenate([ahead, behind]).astype(F32)
        return pick(total, dim, 0).astype(F32) + got

    total_a = term(near, slice(0, part_a))
    first_a = halves(total_a, 0)
    near = after(first_a, near)
    total_b = term(near, slice(part_a, width))
    first_a = both(first_a, 0)
    first_b = both(halves(total_b, 1), 1)
    last_a = relayed(total_a, 0, *first_a)
    first_b = [after(last_a, v) for v in first_b]
    one_a = summed(total_a, 0, *first_a, *both(last_a, 0))[None]
    last_b = both(relayed(total_b, 1, *first_b), 1)
    chunks_a = cut(one_a, 1)
    last_b = [after(chunks_a, v) for v in last_b]
    two_a = send(chunks_a, 1)
    one_b = summed(total_b, 1, *first_b, *last_b)[:, None]
    two_b = send(cut(one_b, 0), 0)
    two_a = gathered(one_a, 1, two_a)[0].astype(F16)
    two_b = [after([two_a], v) for v in two_b]
    two_b = gathered(one_b, 0, two_b)[0].astype(F16)
    two = [two_a, two_b]
    last = jnp.concatenate(two, axis=1).reshape(NZ, rows * width // 128, 128)
    last = lax.all_to_all(last, "z", 0, 0)
    grad = (last.astype(F32).sum(axis=0) * (1.0 / SCALE)).reshape(rows, width)

    moment_s, second_s, weight_s = adamw(grad[:sr], master_shared, moment_shared, second_shared)
    moment_r, second_r, weight_r = adamw(grad[sr:], master_routed, moment_routed, second_routed)

    weight = jnp.concatenate([weight_s, weight_r], axis=0).reshape(1, rows * width // 128, 128)
    weight = lax.all_to_all(jnp.broadcast_to(weight, (NZ,) + weight.shape[1:]), "z", 0, 0)
    mine = weight.reshape(group, width)
    mine_plus, mine_minus = x_ring(mine, 1), x_ring(mine, 3)
    other = y_swap(mine)
    mine_two = x_ring(mine, 2)
    other_plus, other_minus = x_ring(other, 1), x_ring(other, 3)
    other_two = y_swap(mine_two)
    early = jnp.concatenate([mine, mine_plus, mine_minus, other, mine_two], axis=0)
    late = [other_plus, other_minus, other_two]
    slot = jnp.array([0, 1, 4, 2, 3, 5, 7, 6], jnp.int32)

    def wanted(count, low):
        n = 2 * NZ * NX * count
        r = after([weight_s, weight_r], lax.iota(jnp.int32, n))
        back = (x - (r // count) % NX) % NX
        zz = (r // (count * NX)) % NZ
        flip = (r // (count * NX * NZ)) ^ yl
        block = slot[flip * NX + back]
        want = (block * NZ + zz) * rows + low + r % count
        return lax.optimization_barrier(want)

    def take(want, start, full):
        want = lax.optimization_barrier(want - start)
        q = lax.broadcasted_iota(jnp.int32, (want.shape[0], full.shape[0]), 1)
        return dot(lax.optimization_barrier((want[:, None] == q).astype(BF)), full).astype(BF)

    wants = [wanted(sr, 0), wanted(rr, sr)]
    firsts = [take(want, 0, early) for want in wants]
    late = jnp.concatenate([after(firsts, v) for v in late], axis=0)
    shared, routed = (f + take(want, early.shape[0], late) for f, want in zip(firsts, wants))
    return (moment_s, second_s, moment_r, second_r, shared, routed)


def solution(mesh):
    fine = Mesh(mesh.devices.reshape(2, 2, 2, NZ, NX), AXES)
    split = P(AXES, None)
    flat = P(AXES)
    cuts = P(("yh", "core"), None)
    return jax.shard_map(
        local,
        mesh=fine,
        in_specs=(split, split, split, flat, flat) + (split,) * 6,
        out_specs=(split,) * 4 + (cuts,) * 2,
        check_vma=False,
    )
```

```python
import jax
import jax.numpy as jnp
import numpy as np
from jax import lax
from jax.experimental import pallas as pl
from jax.experimental.pallas import tpu as pltpu
from jax.sharding import Mesh, PartitionSpec as P

AXES = ("yh", "core", "yl", "z", "x")
NX, NY, NZ = 4, 4, 8
SCALE = 0.25
BF = jnp.bfloat16
F32 = jnp.float32
F16 = jnp.float16


def adamw(grad, master, moment, second):
    corr_one = 1.0 - 0.9**20
    corr_two = 1.0 - 0.95**20
    new_moment = 0.9 * moment + 0.1 * grad
    new_second = 0.95 * second + 0.05 * grad * grad
    step_dir = new_moment / corr_one / (jnp.sqrt(new_second / corr_two) + 1e-08)
    new_master = master - 0.02 * (step_dir + 0.1 * master)
    return (new_moment, new_second, new_master.astype(BF))


def x_ring(v, d):
    return lax.ppermute(v, "x", [(i, (i + d) % NX) for i in range(NX)])


def y_ring(v, d):
    return lax.ppermute(v, ("yh", "yl"), [(i, (i + d) % NY) for i in range(NY)])


def y_swap(v):
    return lax.ppermute(v, "yl", [(0, 1), (1, 0)])


def core_swap(v):
    return lax.ppermute(v, "core", [(0, 1), (1, 0)])


def after(done, v):
    return lax.optimization_barrier((v, *done))[0]


def row_order(sr, rr):
    rows = sr + rr
    n = NX * 2 * NZ * rows
    xs, ys, zs, i = np.meshgrid(np.arange(NX), np.arange(2), np.arange(NZ), np.arange(rows), indexing="ij")
    dev = (ys * NZ + zs) * NX + xs
    flat = np.arange(n)
    keep = (i < sr).reshape(-1)
    shared = np.zeros((n, 2 * NZ * NX * sr), np.float32)
    shared[flat[keep], (dev * sr + i).reshape(-1)[keep]] = 1
    routed = np.zeros((2, n, 2, 2 * NZ * NX * rr), np.float32)
    for core in range(2):
        routed[core, flat[~keep], core, (dev * rr + i - sr).reshape(-1)[~keep]] = 1
    return shared.astype(BF), routed.reshape(2, n, -1).astype(BF)


def dot_t(a, b):
    return lax.dot_general(a, b, (((1,), (1,)), ((), ())), preferred_element_type=F32)


def dot(a, b):
    return jnp.dot(a, b, preferred_element_type=F32)


def order_kernel(core_ref, count_ref, token_ref, shared_ref, routed_ref, shared_order_ref, routed_order_ref, far, near):
    tok, slots = shared_ref.shape[0], routed_ref.shape[0]
    names = lax.broadcasted_iota(jnp.int32, (tok, slots), 0) == token_ref[...]
    live = lax.broadcasted_iota(jnp.int32, (tok, slots), 1) < count_ref[0]
    place = jnp.where(names & live, 1.0, 0.0).astype(BF)
    slot_rows = dot_t(routed_order_ref[0], routed_ref[...]).astype(BF)
    order = jnp.concatenate([shared_order_ref[...], slot_rows], axis=1)
    total = dot_t(order, jnp.concatenate([shared_ref[...], place], axis=1))

    @pl.when(pl.program_id(0) < 2)
    def _():
        far[...] = total.astype(BF).reshape(far.shape)

    @pl.when(pl.program_id(0) >= 2)
    def _():
        near[...] = total.astype(BF).reshape(near.shape)


def ordered(core, count, token, hid_shared, hid_routed, shared_order, routed_order):
    tok = hid_shared.shape[0]
    slots = hid_routed.shape[0]
    n, cut = shared_order.shape
    pair = routed_order.shape[2]

    def who(j, c):
        return jnp.where(j < 2, 1 - c[0], c[0])

    def out(low):
        return pl.BlockSpec((NX, 1, n // NX, tok), lambda j, c, m: (0, jnp.clip(j - low, 0, 1), 0, 0))

    shape = jax.ShapeDtypeStruct((NX, 2, n // NX, tok), BF)
    return pl.pallas_call(
        order_kernel,
        grid_spec=pltpu.PrefetchScalarGridSpec(
            num_scalar_prefetch=2,
            grid=(4,),
            in_specs=[
                pl.BlockSpec((1, slots), lambda j, c, m: (0, 0)),
                pl.BlockSpec((tok, cut), lambda j, c, m: (0, (j % 2) * 2 + who(j, c))),
                pl.BlockSpec((slots, pair), lambda j, c, m: (0, j % 2)),
                pl.BlockSpec((n, cut), lambda j, c, m: (0, 0)),
                pl.BlockSpec((1, n, pair), lambda j, c, m: (who(j, c), 0, 0)),
            ],
            out_specs=[out(0), out(2)],
        ),
        out_shape=[shape, shape],
        compiler_params=pltpu.CompilerParams(vmem_limit_bytes=56 * 2**20),
        cost_estimate=pl.CostEstimate(flops=16 * n * cut * tok, bytes_accessed=20 * n * tok, transcendentals=0),
    )(core.reshape(1), count, token.reshape(1, slots), hid_shared, hid_routed, shared_order, routed_order)


def local(
    hid_shared,
    hid_routed,
    out_grad,
    slot_token,
    slot_count,
    master_shared,
    moment_shared,
    second_shared,
    master_routed,
    moment_routed,
    second_routed,
):
    tok, width = out_grad.shape
    slots = hid_routed.shape[0]
    sr, rr = master_shared.shape[0], master_routed.shape[0]
    rows = sr + rr
    group = NZ * rows
    core = lax.axis_index("core")
    x = lax.axis_index("x")
    yh, yl = lax.axis_index("yh"), lax.axis_index("yl")
    y = yh * 2 + yl

    shared_order, routed_order = (jnp.asarray(v) for v in row_order(sr, rr))
    part_a = width * 11 // 20
    out_far = core_swap(out_grad)
    far, near = ordered(core, slot_count, slot_token, hid_shared, hid_routed, shared_order, routed_order)
    far = core_swap(far).reshape(-1, tok)
    near = near.reshape(-1, tok)

    def term(near, cols):
        total = dot(near, out_grad[:, cols]) + dot(far, out_far[:, cols])
        return (SCALE * total).astype(F16).reshape(NX, NY, group, -1)

    def pick(v, dim, step):
        index = ((x, y)[dim] + step) % 4
        return lax.dynamic_index_in_dim(v, index, dim, keepdims=False)

    def cut(v, dim):
        return [pick(v, dim, d).astype(F16) for d in (2, 1, 3)]

    def send(chunks, dim):
        return [(x_ring, y_ring)[dim](v, d) for v, d in zip(chunks, (2, 1, 3))]

    def gathered(v, dim, back):
        return sum((b.astype(F32) for b in back), pick(v, dim, 0).astype(F32))

    def front(v):
        return lax.broadcasted_iota(jnp.int32, v.shape, 0) < 2

    def halves(total, dim):
        two, ahead, behind = (pick(total, dim, d) for d in (2, 1, 3))
        return jnp.where(front(two), two, ahead), jnp.where(front(two), behind, two)

    def both(chunks, dim):
        ring = (x_ring, y_ring)[dim]
        return ring(chunks[0], 1), ring(chunks[1], 3)

    def relayed(total, dim, plus, minus):
        ahead = pick(total, dim, 1)[:2].astype(F32) + plus[:2].astype(F32)
        behind = pick(total, dim, 3)[2:].astype(F32) + minus[2:].astype(F32)
        return ahead.astype(F16), behind.astype(F16)

    def summed(total, dim, plus, minus, ahead, behind):
        got = jnp.where(front(plus), minus, plus).astype(F32)
        got = got + jnp.concatenate([ahead, behind]).astype(F32)
        return pick(total, dim, 0).astype(F32) + got

    total_a = term(near, slice(0, part_a))
    first_a = halves(total_a, 0)
    near = after(first_a, near)
    total_b = term(near, slice(part_a, width))
    first_a = both(first_a, 0)
    first_b = both(halves(total_b, 1), 1)
    last_a = relayed(total_a, 0, *first_a)
    first_b = [after(last_a, v) for v in first_b]
    one_a = summed(total_a, 0, *first_a, *both(last_a, 0))[None]
    last_b = both(relayed(total_b, 1, *first_b), 1)
    chunks_a = cut(one_a, 1)
    last_b = [after(chunks_a, v) for v in last_b]
    two_a = send(chunks_a, 1)
    one_b = summed(total_b, 1, *first_b, *last_b)[:, None]
    two_b = send(cut(one_b, 0), 0)
    two_a = gathered(one_a, 1, two_a)[0].astype(F16)
    two_b = [after([two_a], v) for v in two_b]
    two_b = gathered(one_b, 0, two_b)[0].astype(F16)
    two = [two_a, two_b]
    last = jnp.concatenate(two, axis=1).reshape(NZ, rows * width // 128, 128)
    last = lax.all_to_all(last, "z", 0, 0)
    grad = (last.astype(F32).sum(axis=0) * (1.0 / SCALE)).reshape(rows, width)

    moment_s, second_s, weight_s = adamw(grad[:sr], master_shared, moment_shared, second_shared)
    moment_r, second_r, weight_r = adamw(grad[sr:], master_routed, moment_routed, second_routed)

    weight = jnp.concatenate([weight_s, weight_r], axis=0).reshape(1, rows * width // 128, 128)
    weight = lax.all_to_all(jnp.broadcast_to(weight, (NZ,) + weight.shape[1:]), "z", 0, 0)
    mine = weight.reshape(group, width)
    mine_two = x_ring(mine, 2)
    mine_plus, mine_minus = x_ring(mine, 1), x_ring(mine, 3)
    other_two = y_swap(mine_two)
    other = after([mine_two], y_swap(mine))
    other_plus, other_minus = (after([other_two], x_ring(other, d)) for d in (1, 3))
    early = jnp.concatenate([mine, mine_plus, mine_minus, other, mine_two], axis=0)
    late = [other_plus, other_minus, other_two]
    slot = jnp.array([0, 1, 4, 2, 3, 5, 7, 6], jnp.int32)

    def wanted(count, low):
        n = 2 * NZ * NX * count
        r = after([weight_s, weight_r], lax.iota(jnp.int32, n))
        back = (x - (r // count) % NX) % NX
        zz = (r // (count * NX)) % NZ
        flip = (r // (count * NX * NZ)) ^ yl
        block = slot[flip * NX + back]
        want = (block * NZ + zz) * rows + low + r % count
        return lax.optimization_barrier(want)

    def take(want, start, full):
        want = lax.optimization_barrier(want - start)
        q = lax.broadcasted_iota(jnp.int32, (want.shape[0], full.shape[0]), 1)
        return dot(lax.optimization_barrier((want[:, None] == q).astype(BF)), full).astype(BF)

    wants = [wanted(sr, 0), wanted(rr, sr)]
    firsts = [take(want, 0, early) for want in wants]
    late = jnp.concatenate([after(firsts, v) for v in late], axis=0)
    shared, routed = (f + take(want, early.shape[0], late) for f, want in zip(firsts, wants))
    return (moment_s, second_s, moment_r, second_r, shared, routed)


def solution(mesh):
    fine = Mesh(mesh.devices.reshape(2, 2, 2, NZ, NX), AXES)
    split = P(AXES, None)
    flat = P(AXES)
    cuts = P(("yh", "core"), None)
    return jax.shard_map(
        local,
        mesh=fine,
        in_specs=(split, split, split, flat, flat) + (split,) * 6,
        out_specs=(split,) * 4 + (cuts,) * 2,
        check_vma=False,
    )
```
